1024 devices in a mesh: win: 16 (over z_lo), tile: 64 (over y, x, z_hi, core).
Axes of the slice: x: 4, y: 4, z: 32 (z_hi: 2, z_lo: 16; z = z_hi * 16 + z_lo), core: 2. Of those that a mesh axis runs over, the one named last changes fastest.
Arguments:
- increment: float32 [16, 72, 384, 768], P('win', None, 'tile'), may hold values from -6 to 6
- background: float32 [72, 384, 768], P(None, 'tile'), may hold values from -6 to 6
- lat_diffusion: float32 [16, 384, 768], P('win', 'tile'), may hold values from 0.05 to 0.2
- lon_diffusion: float32 [16, 384, 768], P('win', 'tile'), may hold values from 0.1 to 0.2
- advection: float32 [16, 384, 768], P('win', 'tile'), may hold values from -0.4 to 0.4
- spectrum: float32 [512, 384], P('tile'), may hold values from 0.3 to 3
- obs_index: int32 [16, 32768], P('win', 'tile'), may hold values from 0 to 331775
- obs_count: int32 [16, 64], P('win', 'tile'), may hold values from 1 to 512, as said below
- innovation: float32 [16, 32768], P('win', 'tile'), may hold values from -6 to 6
- obs_precision: float32 [16, 32768], P('win', 'tile'), may hold values from 0.25 to 2
Outputs:
- gradient: float32 [16, 72, 384, 768], P('win', None, 'tile')
The draws below stay inside these ranges and needn't reach their ends.
Inputs may be any that keep to these rules, and one draw needn't show every extreme that they name: `obs_index`: each entry is level * 6 * 768 + row * 768 + longitude, counted within the rows of its own tile. Only the first obs_count[w, t] slots of tile t's block of a sub-window are live; in every draw some tile of some sub-window has all 512 live.
All inputs are finite; a program needn't handle non-finite values.
Results may differ from the reference program's by a relative error of at most 0.000062.
Values sent between devices are 32-bit elements; how exact they have to be, the bound alone decides.
A program may use at most 32 MiB of HBM per device.

```python
import math
import jax
import jax.numpy as jnp
from jax import lax

LEV = 72
LON = 768
ROWS = 6
OBS_DEV = 512
NWIN = 16
TILES = 64
NLAT = 384
KEEP = 512
CELLS = 331776


def draw_obs_count(key, part):
    count_key, place_key = jax.random.split(jax.random.fold_in(key, 7))
    counts = jax.random.randint(count_key, (NWIN * TILES,), 1, OBS_DEV + 1)
    full_at = jax.random.randint(place_key, (), 0, NWIN * TILES)
    counts = counts.at[full_at].set(OBS_DEV)
    return counts.reshape(NWIN, TILES).astype(jnp.int32)


def plant(entries, stream_key, low, largest):
    longest = entries.shape.index(max(entries.shape))
    spots = []
    for shift in (0, 1):
        where = [jax.random.randint(jax.random.fold_in(stream_key, axis), (), 0, length) for axis, length in enumerate(entries.shape)]
        where[longest] = (where[longest] + shift) % entries.shape[longest]
        spots.append(tuple(where))
    return entries.at[spots[0]].set(low).at[spots[1]].set(largest)


def levels(rng, shape, pieces, low, top_value):
    def one(dim, blocks):
        draws = jax.random.uniform(jax.random.fold_in(jax.random.fold_in(rng, 6), dim), (blocks,), jnp.float32, low / len(pieces), top_value / len(pieces))
        return jnp.repeat(jnp.exp(draws), shape[dim] // blocks).reshape((-1,) + (1,) * (len(shape) - dim - 1))

    gain = one(*pieces[0])
    for cut in pieces[1:]:
        gain = gain * one(*cut)
    return gain


def gaussian(own_key, dims, scale, reach, cuts=(), kind=jnp.bfloat16):
    result = scale * jax.random.normal(own_key, dims, jnp.float32)
    if cuts:
        result = result * levels(own_key, dims, cuts, -0.22, 0.18)
    return jnp.clip(result, -reach, reach).astype(kind)


def setup_inputs(seed: int = 0) -> dict:
    seeds = jax.random.split(jax.random.key(seed), 11)
    return {
        "increment": gaussian(seeds[0], (NWIN, LEV, NLAT, LON), 1.0, 6.0, ((0, 16), (2, 64)), jnp.float32),
        "background": gaussian(seeds[1], (LEV, NLAT, LON), 1.0, 6.0, ((1, 64),), jnp.float32),
        "lat_diffusion": jnp.clip(0.05 + 0.15 * jax.random.uniform(seeds[2], (NWIN, NLAT, LON), jnp.float32) ** levels(seeds[2], (NWIN, NLAT, LON), ((0, 16), (1, 64)), -0.2, 0.2), 0.05, 0.2),
        "lon_diffusion": jnp.clip(0.1 + 0.1 * jax.random.uniform(seeds[3], (NWIN, NLAT, LON), jnp.float32) ** levels(seeds[3], (NWIN, NLAT, LON), ((0, 16), (1, 64)), -0.2, 0.2), 0.1, 0.2),
        "advection": jnp.clip(jax.random.uniform(seeds[4], (NWIN, NLAT, LON), jnp.float32, -0.4, 0.4) * levels(seeds[4], (NWIN, NLAT, LON), ((0, 16), (1, 64)), -0.4, 0.0), -0.4, 0.4),
        "spectrum": jnp.clip(jnp.exp(math.log(3.0) - 2.3025851 * jax.random.uniform(seeds[5], (KEEP, NLAT), jnp.float32) ** levels(seeds[5], (KEEP, NLAT), ((0, 64),), -0.2, 0.2)), 0.3, 3.0),
        "obs_index": plant(jax.random.randint(seeds[6], (NWIN, TILES * OBS_DEV), 0, CELLS), jax.random.fold_in(seeds[6], 1), 0, CELLS - 1).astype(jnp.int32),
        "obs_count": draw_obs_count(jax.random.fold_in(seeds[10], 71), 0),
        "innovation": gaussian(seeds[8], (NWIN, TILES * OBS_DEV), 1.0, 6.0, ((0, 16), (1, 64)), jnp.float32),
        "obs_precision": jnp.clip(jnp.exp(math.log(2.0) - 2.0794415 * jax.random.uniform(seeds[9], (NWIN, TILES * OBS_DEV), jnp.float32) ** levels(seeds[9], (NWIN, TILES * OBS_DEV), ((0, 16), (1, 64)), -0.2, 0.2)), 0.25, 2.0),
    }


def longitude_basis(width, kept):
    half = kept // 2
    wave = jnp.arange(kept, dtype=jnp.int32)
    places = jnp.arange(width, dtype=jnp.int32)
    number = jnp.where(wave < half, wave, wave - half + 1)
    phase = number[:, None] * places[None, :] % width
    angle = 2.0 * jnp.pi * phase.astype(jnp.float32) / width
    scale = jnp.where(wave == 0, jnp.sqrt(1.0 / width), jnp.sqrt(2.0 / width)).astype(jnp.float32)
    table = jnp.where((wave < half)[:, None], jnp.cos(angle), jnp.sin(angle))
    return table * scale[:, None]

def latitude_basis(height):
    modes = jnp.arange(height, dtype=jnp.int32)
    phase = modes[:, None] * (2 * modes[None, :] + 1) % (4 * height)
    angle = jnp.pi * phase.astype(jnp.float32) / (2.0 * height)
    scale = jnp.where(modes == 0, jnp.sqrt(1.0 / height), jnp.sqrt(2.0 / height)).astype(jnp.float32)
    return jnp.cos(angle) * scale[:, None]

def tl_step(center, north, south, lat_coef, lon_coef, drift):
    east = jnp.roll(center, -1, axis=2)
    west = jnp.roll(center, 1, axis=2)
    return (1.0 - 2.0 * lat_coef - 2.0 * lon_coef) * center + lat_coef * (north + south) + (lon_coef - 0.5 * drift) * east + (lon_coef + 0.5 * drift) * west

def shifted_rows(field):
    zero_row = jnp.zeros_like(field[:, :1])
    north = jnp.concatenate([field[:, 1:], zero_row], axis=1)
    south = jnp.concatenate([zero_row, field[:, :-1]], axis=1)
    return (north, south)

def forward_two(packed):
    field, lat_coef, lon_coef, drift = packed
    for repeat in range(2):
        north, south = shifted_rows(field)
        field = tl_step(field, north, south, lat_coef, lon_coef, drift)
    return field

def adjoint_step(field, lat_coef, lon_coef, drift):
    weighted = lat_coef * field
    north, south = shifted_rows(weighted)
    eastward = (lon_coef - 0.5 * drift) * field
    westward = (lon_coef + 0.5 * drift) * field
    return (1.0 - 2.0 * lat_coef - 2.0 * lon_coef) * field + north + south + jnp.roll(eastward, 1, axis=2) + jnp.roll(westward, -1, axis=2)

def adjoint_two(packed):
    field, lat_coef, lon_coef, drift = packed
    for repeat in range(2):
        field = adjoint_step(field, lat_coef, lon_coef, drift)
    return field

def reference(increment, background, lat_diffusion, lon_diffusion, advection, spectrum, obs_index, obs_count, innovation, obs_precision):
    highest = lax.Precision.HIGHEST
    zonal = longitude_basis(LON, KEEP)
    merid = latitude_basis(NLAT)
    propagated = lax.map(forward_two, (increment, lat_diffusion, lon_diffusion, advection))
    prior = jnp.concatenate([background[None], propagated[:-1]], axis=0)

    def precision(pair):
        mismatch = pair[0] - pair[1]
        coef = jnp.einsum('kx,lnx->kln', zonal, mismatch, precision=highest)
        modal = jnp.einsum('kln,mn->klm', coef, merid, precision=highest) * spectrum[:, None, :]
        back = jnp.einsum('klm,mn->kln', modal, merid, precision=highest)
        return jnp.einsum('kx,kln->lnx', zonal, back, precision=highest)
    multiplier = lax.map(precision, (increment, prior))
    slots = jnp.arange(TILES * OBS_DEV, dtype=jnp.int32)
    tile_of = slots // OBS_DEV
    live = (slots % OBS_DEV)[None, :] < obs_count[:, tile_of]
    level = obs_index // (ROWS * LON)
    remain = obs_index % (ROWS * LON)
    row_at = remain // LON + (tile_of * ROWS)[None, :]
    column = remain % LON
    window = jnp.broadcast_to(jnp.arange(NWIN, dtype=jnp.int32)[:, None], obs_index.shape)
    values = propagated[window, level, row_at, column]
    departure = jnp.where(live, obs_precision * (values - innovation), jnp.zeros_like(innovation))
    placed = jnp.zeros_like(increment).at[window, level, row_at, column].add(departure)
    later = jnp.concatenate([multiplier[1:], jnp.zeros_like(multiplier[:1])], axis=0)
    forcing = later - placed
    adjoint = lax.map(adjoint_two, (forcing, lat_diffusion, lon_diffusion, advection))
    return multiplier - adjoint
```

```python
import jax
import jax.numpy as jnp
import ml_dtypes
import numpy as np
from jax import lax
from jax.experimental import pallas as pl
from jax.experimental.pallas import tpu as pltpu
from jax.sharding import PartitionSpec as P

LEV, LON, ROWS, KEEP, NLAT, TILES, NWIN = 72, 768, 6, 512, 384, 64, 16
EXT = 8
PLANE = LEV * LON
UNITS = 5
VMEM_LIMIT = 40 * 1024 * 1024


def zonal_table():
    half = KEEP // 2
    wave = np.arange(KEEP)
    number = np.where(wave < half, wave, wave - half + 1)
    phase = number[:, None] * np.arange(LON)[None, :] % LON
    angle = 2.0 * np.pi * phase / LON
    scale = np.where(wave == 0, np.sqrt(1.0 / LON), np.sqrt(2.0 / LON))
    return np.where((wave < half)[:, None], np.cos(angle), np.sin(angle)) * scale[:, None]


def meridional_table():
    modes = np.arange(NLAT)
    phase = modes[:, None] * (2 * modes[None, :] + 1) % (4 * NLAT)
    scale = np.where(modes == 0, np.sqrt(1.0 / NLAT), np.sqrt(2.0 / NLAT))
    return np.cos(np.pi * phase / (2.0 * NLAT)) * scale[:, None]


def extended_meridional():
    table = meridional_table()
    out = np.zeros((NLAT, TILES, EXT))
    for tile in range(TILES):
        for i in range(EXT):
            row = tile * ROWS + (i if tile % 2 else ROWS - 1 - i)
            if 0 <= row < NLAT:
                out[:, tile, i] = table[:, row]
    return out.reshape(NLAT, TILES * EXT)


def two_parts(table):
    high = table.astype(ml_dtypes.bfloat16)
    low = (table - high.astype(np.float64)).astype(ml_dtypes.bfloat16)
    return high, low


def split(x):
    high = x.astype(jnp.bfloat16)
    low = (x - high.astype(jnp.float32)).astype(jnp.bfloat16)
    return high, low


def dot(a, b):
    return jnp.dot(a, b, preferred_element_type=jnp.float32)


def dot3(a, b):
    return dot(a[0], b[0]) + (dot(a[0], b[1]) + dot(a[1], b[0]))


def source_row(core, i):
    return jnp.where(core == 0, ROWS - 1 - i, i)


def project_kernel(flags, inc, bg, zh, zl, out):
    core = flags[0]
    first = (flags[1] == 0).astype(jnp.float32)
    field = inc[...] - first * bg[...]
    coefs = dot3(split(field.reshape(ROWS * LEV, LON)), (zh[...], zl[...]))
    coefs = coefs.reshape(ROWS, LEV, KEEP)
    for i in range(ROWS):
        out[source_row(core, i)] = coefs[i]


def coef_rows(core, lat, lon, drift, inner, outer):
    def pick(own, near, far):
        def get(r):
            if r < 0:
                return inner[near[-1 - r], :][None, :]
            if r >= ROWS:
                return outer[far[r - ROWS], :][None, :]
            return own[pl.ds(source_row(core, r), 1), :]

        return get

    return pick(lat, (0, 1), (0, 1)), pick(lon, (2,), (2,)), pick(drift, (3,), (3,))


def weights(a, b, c):
    return 1.0 - 2.0 * a - 2.0 * b, b - 0.5 * c, b + 0.5 * c


def forward_kernel(flags, inc, near, lat, lon, drift, inner, outer, zh, zl, p_out, y_out, mid):
    core = flags[0]
    la, lo, dr = coef_rows(core, lat, lon, drift, inner, outer)

    def state(r):
        if r < 0:
            return near[-1 - r]
        return inc[source_row(core, r)]

    def step(get, r, lowest, highest):
        a = la(r)
        if r > highest:
            return a * get(r - 1)
        cen, east, west = weights(a, lo(r), dr(r))
        mine = get(r)
        beside = get(r - 1)
        if r < highest:
            beside = beside + get(r + 1)
        return (
            cen * mine
            + a * beside
            + east * pltpu.roll(mine, LON - 1, 1)
            + west * pltpu.roll(mine, 1, 1)
        )

    for r in range(-1, ROWS + 1):
        mid[r + 1] = step(state, r, -2, ROWS - 1)
    for r in range(EXT):
        p_out[r] = step(lambda q: mid[q + 1], r, -1, ROWS)
    y = dot3(split(p_out[...].reshape(EXT * LEV, LON)), (zh[...], zl[...]))
    y_out[...] = y.reshape(EXT, LEV, KEEP)


def unit_base(i, quarter, block):
    return quarter * 640 + (block % 2) * 40 + (block // 2) * 8 + i


def arrange_kernel(flags, shifted, y, out):
    keep = (flags[1] != NWIN - 1).astype(jnp.float32)
    for quarter in range(4):
        for slot in range(8):
            base = quarter * 640 + slot * 80 + 40 + 32
            out[base : base + 8, :] = jnp.zeros((8, 128), jnp.float32)
    for i in range(EXT):
        coefs = -keep * y[i]
        if i < ROWS:
            coefs = shifted[i] + coefs
        for quarter in range(4):
            for block in range(9):
                out[pl.ds(unit_base(i, quarter, block), 8, stride=80), :] = coefs[
                    block * 8 : block * 8 + 8, quarter * 128 : quarter * 128 + 128
                ]


def modal_kernel(got, spec, ph, pl_, qh, ql, out):
    data = got[...].reshape(TILES, UNITS, EXT, 128)
    x = jnp.concatenate([data[:, u].reshape(TILES * EXT, 128) for u in range(UNITS)], axis=1)
    modal = dot3((ph[...], pl_[...]), split(x))
    scale = spec[...].T
    modal = modal * jnp.concatenate([scale] * UNITS, axis=1)
    back = dot3((qh[...], ql[...]), split(modal))
    for u in range(UNITS):
        out[:, u * 8 : u * 8 + 8, :] = back[:, u * 128 : u * 128 + 128].reshape(TILES, EXT, 128)


def collect_kernel(got, own, far):
    for i in range(EXT):
        for quarter in range(4):
            for block in range(9):
                tile = got[pl.ds(unit_base(i, quarter, block), 8, stride=80), :]
                rows = pl.ds(block * 8, 8)
                lanes = pl.ds(quarter * 128, 128)
                if i < ROWS:
                    own[i, rows, lanes] = tile
                else:
                    far[i - ROWS, rows, lanes] = tile


def forcing_kernel(flags, own, far, placed, zh, zl, out):
    keep = (flags[1] != NWIN - 1).astype(jnp.float32)
    table = (zh[...], zl[...])
    field = dot3(split(own[...].reshape(ROWS * LEV, KEEP)), table).reshape(ROWS, LEV, LON)
    out[:ROWS] = keep * field - placed[:ROWS]
    field = dot3(split(far[...].reshape(2 * LEV, KEEP)), table).reshape(2, LEV, LON)
    out[ROWS:] = keep * field - placed[ROWS:]


def adjoint_kernel(flags, force, near, lat, lon, drift, inner, outer, out, mid):
    core = flags[0]
    la, lo, dr = coef_rows(core, lat, lon, drift, inner, outer)

    def start(r):
        if r < 0:
            return near[-1 - r]
        return force[r]

    def step(get, r):
        cen, east, west = weights(la(r), lo(r), dr(r))
        mine = get(r)
        return (
            cen * mine
            + la(r + 1) * get(r + 1)
            + la(r - 1) * get(r - 1)
            + pltpu.roll(east * mine, 1, 1)
            + pltpu.roll(west * mine, LON - 1, 1)
        )

    for r in range(-1, ROWS + 1):
        mid[r + 1] = step(start, r)
    for r in range(ROWS):
        out[r] = step(lambda q: mid[q + 1], r)


def finish_kernel(flags, shifted, adjoint, zh, zl, out):
    core = flags[0]
    field = dot3(split(shifted[...].reshape(ROWS * LEV, KEEP)), (zh[...], zl[...]))
    field = field.reshape(ROWS, LEV, LON)
    for i in range(ROWS):
        out[source_row(core, i)] = field[i] - adjoint[i]


def call(kernel, shapes, args, scratch=(), scalar=True, cost=None):
    specs = [pl.BlockSpec(memory_space=pltpu.VMEM)] * len(args)
    if scalar:
        specs[0] = pl.BlockSpec(memory_space=pltpu.SMEM)
    shapes = [jax.ShapeDtypeStruct(s, jnp.float32) for s in shapes]
    single = len(shapes) == 1
    return pl.pallas_call(
        kernel,
        out_shape=shapes[0] if single else shapes,
        in_specs=specs,
        out_specs=(
            pl.BlockSpec(memory_space=pltpu.VMEM)
            if single
            else [pl.BlockSpec(memory_space=pltpu.VMEM)] * len(shapes)
        ),
        scratch_shapes=[pltpu.VMEM(s, jnp.float32) for s in scratch],
        compiler_params=pltpu.CompilerParams(vmem_limit_bytes=VMEM_LIMIT),
        cost_estimate=pl.CostEstimate(
            flops=cost or 10_000_000, bytes_accessed=4_000_000, transcendentals=0
        ),
    )(*args)


def body(
    increment,
    background,
    lat_diffusion,
    lon_diffusion,
    advection,
    spectrum,
    obs_index,
    obs_count,
    innovation,
    obs_precision,
):
    tile = lax.axis_index("tile")
    core = tile % 2
    window = lax.axis_index("win")
    flags = jnp.stack([core, window]).astype(jnp.int32)
    inner_pairs = [(t, t ^ 1) for t in range(TILES)]
    outer_pairs = [(t, t + 1 if t % 2 else t - 1) for t in range(1, TILES - 1)]
    earlier = [(w, (w - 1) % NWIN) for w in range(NWIN)]
    later = [(w, (w + 1) % NWIN) for w in range(NWIN)]

    zonal = zonal_table()
    zonal_back = two_parts(zonal)
    zonal_fwd = tuple(np.ascontiguousarray(part.T) for part in zonal_back)
    merid = extended_meridional()
    merid_fwd = two_parts(merid)
    merid_back = tuple(np.ascontiguousarray(part.T) for part in merid_fwd)

    inc = increment[0].transpose(1, 0, 2)
    bg = background.transpose(1, 0, 2)
    lat, lon, drift = lat_diffusion[0], lon_diffusion[0], advection[0]

    def in_order(rows):
        return jnp.where(core == 0, rows[::-1], rows)

    coefs = call(project_kernel, [(ROWS, LEV, KEEP)], (flags, inc, bg, *zonal_fwd), cost=10**9)
    shifted = lax.ppermute(coefs, "win", earlier)

    near = lax.ppermute(jnp.where(core == 0, inc[:3:-1], inc[:2]), "tile", inner_pairs)
    lat_o, lon_o, drift_o = in_order(lat), in_order(lon), in_order(drift)
    inner = lax.ppermute(
        jnp.stack([lat_o[0], lat_o[1], lon_o[0], drift_o[0]]), "tile", inner_pairs
    )
    cells = obs_index[0]
    live = jnp.arange(cells.shape[0], dtype=jnp.int32) < obs_count[0, 0]
    rest = cells % (ROWS * LON)
    row = rest // LON
    place = jnp.where(core == 0, ROWS - 1 - row, row)
    own_at = (place * LEV + cells // (ROWS * LON)) * LON + rest % LON
    sent = jnp.where(live, own_at, 0).astype(jnp.float32)
    outer = lax.ppermute(
        jnp.concatenate([lat_o[5], lat_o[4], lon_o[5], drift_o[5], sent]), "tile", outer_pairs
    )
    far_cells = outer[4 * LON :].astype(jnp.int32)
    outer = outer[: 4 * LON].reshape(4, LON)
    edge = far_cells >= 4 * PLANE
    far_at = (11 - far_cells // PLANE) * PLANE + far_cells % PLANE

    p, y = call(
        forward_kernel,
        [(EXT, LEV, LON), (EXT, LEV, KEEP)],
        (flags, inc, near, lat, lon, drift, inner, outer, *zonal_fwd),
        scratch=[(EXT, LEV, LON)],
        cost=10**9,
    )
    send = call(arrange_kernel, [(TILES * UNITS * EXT, 128)], (flags, shifted, y))
    send = send.reshape(TILES, UNITS * EXT, 128)
    groups = [list(range(g * 16, g * 16 + 16)) for g in range(4)]
    spec = lax.all_gather(spectrum, "tile", axis_index_groups=groups, tiled=True)
    got = lax.all_to_all(send, "tile", split_axis=0, concat_axis=0, tiled=True)

    found = p.reshape(-1)[jnp.concatenate([own_at, jnp.where(edge, far_at, 0)])]
    values = found[:512] + lax.ppermute(
        jnp.where(edge, found[512:], 0.0), "tile", outer_pairs
    )
    departure = jnp.where(
        live, obs_precision[0] * (values - innovation[0]), jnp.zeros_like(values)
    )
    far_departure = lax.ppermute(departure, "tile", outer_pairs)
    placed = (
        jnp.zeros((EXT * PLANE,), jnp.float32)
        .at[jnp.concatenate([own_at, jnp.where(edge, far_at, EXT * PLANE)])]
        .add(jnp.concatenate([departure, far_departure]), mode="drop")
        .reshape(EXT, LEV, LON)
    )

    back = call(
        modal_kernel,
        [(TILES, UNITS * EXT, 128)],
        (got, spec, *merid_fwd, *merid_back),
        scalar=False,
        cost=10**9,
    )
    grid = lax.all_to_all(back, "tile", split_axis=0, concat_axis=0, tiled=True)
    own, far = call(
        collect_kernel,
        [(ROWS, LEV, KEEP), (2, LEV, KEEP)],
        (grid.reshape(TILES * UNITS * EXT, 128),),
        scalar=False,
    )
    at_home = lax.ppermute(own, "win", later)
    force = call(
        forcing_kernel, [(EXT, LEV, LON)], (flags, own, far, placed, *zonal_back), cost=10**9
    )
    force_near = lax.ppermute(force[:2], "tile", inner_pairs)
    adjoint = call(
        adjoint_kernel,
        [(ROWS, LEV, LON)],
        (flags, force, force_near, lat, lon, drift, inner, outer),
        scratch=[(EXT, LEV, LON)],
    )
    gradient = call(
        finish_kernel, [(ROWS, LEV, LON)], (flags, at_home, adjoint, *zonal_back), cost=10**9
    )
    return gradient.transpose(1, 0, 2)[None]


def solution(mesh):
    in_specs = (
        P("win", None, "tile", None),
        P(None, "tile", None),
        P("win", "tile", None),
        P("win", "tile", None),
        P("win", "tile", None),
        P("tile", None),
        P("win", "tile"),
        P("win", "tile"),
        P("win", "tile"),
        P("win", "tile"),
    )
    out_specs = P("win", None, "tile", None)
    return jax.shard_map(body, mesh=mesh, in_specs=in_specs, out_specs=out_specs, check_vma=False)
```

```python
import jax
import jax.numpy as jnp
import ml_dtypes
import numpy as np
from jax import lax
from jax.experimental import pallas as pl
from jax.experimental.pallas import tpu as pltpu
from jax.sharding import PartitionSpec as P

LEV, LON, ROWS, KEEP, NLAT, TILES, NWIN = 72, 768, 6, 512, 384, 64, 16
EXT = 8
UNITS = 5
VMEM_LIMIT = 58 * 1024 * 1024
SLOTS = 512
CELL_ROWS = EXT * LEV


def zonal_table():
    half = KEEP // 2
    wave = np.arange(KEEP)
    number = np.where(wave < half, wave, wave - half + 1)
    phase = number[:, None] * np.arange(LON)[None, :] % LON
    angle = 2.0 * np.pi * phase / LON
    scale = np.where(wave == 0, np.sqrt(1.0 / LON), np.sqrt(2.0 / LON))
    return np.where((wave < half)[:, None], np.cos(angle), np.sin(angle)) * scale[:, None]


def meridional_table():
    modes = np.arange(NLAT)
    phase = modes[:, None] * (2 * modes[None, :] + 1) % (4 * NLAT)
    scale = np.where(modes == 0, np.sqrt(1.0 / NLAT), np.sqrt(2.0 / NLAT))
    return np.cos(np.pi * phase / (2.0 * NLAT)) * scale[:, None]


def extended_meridional():
    table = meridional_table()
    out = np.zeros((NLAT, TILES, EXT))
    for tile in range(TILES):
        for i in range(EXT):
            row = tile * ROWS + (i if tile % 2 else ROWS - 1 - i)
            if 0 <= row < NLAT:
                out[:, tile, i] = table[:, row]
    return out.reshape(NLAT, TILES * EXT)


def two_parts(table):
    high = table.astype(ml_dtypes.bfloat16)
    low = (table - high.astype(np.float64)).astype(ml_dtypes.bfloat16)
    return high, low


def split(x):
    high = x.astype(jnp.bfloat16)
    low = (x - high.astype(jnp.float32)).astype(jnp.bfloat16)
    return high, low


def dot(a, b):
    return jnp.dot(a, b, preferred_element_type=jnp.float32)


def dot3(a, b):
    return dot(a[0], b[0]) + (dot(a[0], b[1]) + dot(a[1], b[0]))


def dot_nt(a, b):
    return lax.dot_general(a, b, (((1,), (1,)), ((), ())), preferred_element_type=jnp.float32)


def dot3_nt(a, b):
    return dot_nt(a[0], b[0]) + (dot_nt(a[0], b[1]) + dot_nt(a[1], b[0]))


def weights(a, b, c):
    return 1.0 - 2.0 * a - 2.0 * b, b - 0.5 * c, b + 0.5 * c


def unit_base(i, quarter, block):
    return quarter * 640 + (block % 2) * 40 + (block // 2) * 8 + i


SHIFT, LAMBDA, HALO, PACK_IN, PACK_OUT, OBS, FOUND, DEPART, SPEC, FORCE = range(10)


def kernel(
    inc,
    bg,
    lat,
    lon,
    drift,
    spectrum,
    cells,
    count,
    innovation,
    precision,
    zh,
    zl,
    ph,
    plo,
    qh,
    ql,
    out,
    coefs,
    shifted,
    near,
    pack,
    pack_in,
    pack_out,
    obs,
    obs_far,
    found,
    found_far,
    depart,
    depart_far,
    spec,
    p,
    mid,
    y,
    send,
    got,
    hot_x,
    hot_r,
    lam,
    lam_near,
    force,
    force_near,
    misc_s,
    misc_r,
    spec_s,
    spec_r,
    fwd_s,
    fwd_r,
    bwd_s,
    bwd_r,
    send2,
    got2,
):
    me = lax.axis_index("tile")
    win = lax.axis_index("win")
    core = me % 2
    half = (me // 2) % 2
    xx = (me // 4) % 4
    yy = me // 16
    inside = jnp.logical_and(me > 0, me < TILES - 1)
    partner = me + 1 - 2 * core
    outer = me + 2 * core - 1
    before = (win + NWIN - 1) % NWIN
    after = (win + 1) % NWIN

    def copy(src, dst, ssem, rsem, window, tile):
        return pltpu.make_async_remote_copy(
            src_ref=src,
            dst_ref=dst,
            send_sem=ssem,
            recv_sem=rsem,
            device_id=(window, tile),
            device_id_type=pl.DeviceIdType.MESH,
        )

    def misc(k, src, dst, window, tile):
        return copy(src, dst, misc_s.at[k], misc_r.at[k], window, tile)

    barrier = pltpu.get_barrier_semaphore()

    def greet(j, carry):
        pl.semaphore_signal(
            barrier,
            inc=1,
            device_id=(win, (me + j) % TILES),
            device_id_type=pl.DeviceIdType.MESH,
        )
        return carry

    for window in (before, after):
        pl.semaphore_signal(
            barrier, inc=1, device_id=(window, me), device_id_type=pl.DeviceIdType.MESH
        )
    lax.fori_loop(1, TILES, greet, 0)

    def src(i):
        return core * i + (1 - core) * (ROWS - 1 - i)

    pack[...] = jnp.zeros_like(pack)
    for k, (ref, i) in enumerate(
        ((lat, 0), (lat, 1), (lon, 0), (drift, 0), (lat, 5), (lat, 4), (lon, 5), (drift, 5))
    ):
        pack[k : k + 1, :] = ref[pl.ds(src(i), 1), :]
    spec[xx, half, core] = spectrum[...]

    number = cells[...].astype(jnp.float32)
    level = jnp.floor((number + 0.5) * (1.0 / (ROWS * LON)))
    rest = number - level * (ROWS * LON)
    row = jnp.floor((rest + 0.5) * (1.0 / LON))
    place = jnp.where(core == 0, ROWS - 1 - row, row)
    slot = lax.broadcasted_iota(jnp.int32, (1, SLOTS), 1)
    live = slot < count[...]
    obs[0:1, :] = jnp.where(live, place * LEV + level, -1.0)
    obs[1:2, :] = rest - row * LON

    @pl.when(jnp.logical_not(inside))
    def _():
        pack_out[...] = jnp.zeros_like(pack_out)
        obs_far[...] = jnp.zeros_like(obs_far)
        found_far[...] = jnp.zeros_like(found_far)
        depart_far[...] = jnp.zeros_like(depart_far)

    first = jnp.where(win == 0, 1.0, 0.0).astype(jnp.float32)
    table = (zh[...], zl[...])
    field = inc[...] - first * bg[...]
    own = dot3(split(field.reshape(ROWS * LEV, LON)), table).reshape(ROWS, LEV, KEEP)
    for i in range(ROWS):
        coefs[src(i)] = own[i]

    pl.semaphore_wait(barrier, TILES + 1)

    shift = misc(SHIFT, coefs, shifted, before, me)
    pack_inner = misc(PACK_IN, pack, pack_in, win, partner)
    pack_outer = misc(PACK_OUT, pack, pack_out, win, outer)
    cells_outer = misc(OBS, obs, obs_far, win, outer)
    spec_across = misc(
        SPEC, spec.at[xx, half, core], spec.at[xx, half, core], win, me + 2 - 4 * half
    )
    rim = (1 - core) * (ROWS - 2)
    halo = misc(HALO, inc.at[pl.ds(rim, 2)], near, win, partner)
    pack_inner.start()
    halo.start()

    @pl.when(inside)
    def _():
        pack_outer.start()
        cells_outer.start()

    shift.start()
    spec_across.start()

    pack_inner.wait()
    halo.wait()

    @pl.when(inside)
    def _():
        pack_outer.wait()

    def la(r):
        if r < 0:
            return pack_in[-1 - r : -r, :]
        if r >= ROWS:
            return pack_out[r - 2 : r - 1, :]
        return lat[pl.ds(src(r), 1), :]

    def lo(r):
        if r < 0:
            return pack_in[2:3, :]
        if r >= ROWS:
            return pack_out[6:7, :]
        return lon[pl.ds(src(r), 1), :]

    def dr(r):
        if r < 0:
            return pack_in[3:4, :]
        if r >= ROWS:
            return pack_out[7:8, :]
        return drift[pl.ds(src(r), 1), :]

    def beyond(r):
        return near[core + (1 - 2 * core) * (-1 - r)]

    def state(r):
        return beyond(r) if r < 0 else inc[src(r)]

    def step(get, r, highest):
        a = la(r)
        if r > highest:
            return a * get(r - 1)
        cen, east, west = weights(a, lo(r), dr(r))
        mine = get(r)
        beside = get(r - 1)
        if r < highest:
            beside = beside + get(r + 1)
        return (
            cen * mine
            + a * beside
            + east * pltpu.roll(mine, LON - 1, 1)
            + west * pltpu.roll(mine, 1, 1)
        )

    for r in range(-1, ROWS + 1):
        mid[r + 1] = step(state, r, ROWS - 1)
    for r in range(EXT):
        p[r] = step(lambda q: mid[q + 1], r, ROWS)
    parts = split(p[...].reshape(CELL_ROWS, LON))
    y[...] = dot3(parts, table).reshape(EXT, LEV, KEEP)

    spec_across.wait()

    def spec_copy(j):
        return copy(
            spec.at[xx, :, core],
            spec.at[xx, :, core],
            spec_s.at[j],
            spec_r.at[xx * 2 + core],
            win,
            yy * 16 + (xx + j // 2) % 4 * 4 + half * 2 + (core + j % 2) % 2,
        )

    for j in range(1, 8):
        spec_copy(j).start()

    shift.wait()
    keep = jnp.where(win == NWIN - 1, 0.0, 1.0).astype(jnp.float32)
    for i in range(EXT):
        c = -keep * y[i]
        if i < ROWS:
            c = shifted[i] + c
        for quarter in range(4):
            for block in range(9):
                send[pl.ds(unit_base(i, quarter, block), 8, stride=80), :] = c[
                    block * 8 : block * 8 + 8, quarter * 128 : quarter * 128 + 128
                ]

    def rows_of(core_there):
        return 40 if core_there == 0 else 32

    def block(ref, t, rows):
        return ref.at[pl.ds(t * 40, rows), :]

    def fwd(d, s, rows):
        return copy(block(send, d, rows), block(got, s, rows), fwd_s.at[d], fwd_r.at[s], win, d)

    def bwd(d, s, rows):
        return copy(block(send2, d, rows), block(got2, s, rows), bwd_s.at[d], bwd_r.at[s], win, d)

    def all_tiles(act, dest_core, dh, skip_self):
        def one(j, carry):
            d = (yy + j // 4) % 4 * 16 + (xx + j % 4) % 4 * 4 + (half + dh) % 2 * 2 + dest_core
            if skip_self:
                pl.when(d != me)(lambda: act(d))
            else:
                act(d)
            return carry

        lax.fori_loop(0, 16, one, 0)

    for dh in (1, 0):
        for there in (0, 1):
            rows = rows_of(there)
            all_tiles(lambda d: fwd(d, me, rows).start(), there, dh, dh == 0)
    got[pl.ds(me * 40, 40), :] = send[pl.ds(me * 40, 40), :]

    @pl.when(inside)
    def _():
        cells_outer.wait()

    far_r = obs_far[0:1, :]
    far_r = jnp.where(
        far_r >= 5.0 * LEV, far_r + LEV, jnp.where(far_r >= 4.0 * LEV, far_r + 3.0 * LEV, -1.0)
    )
    spot_r = jnp.concatenate([obs[0:1, :], far_r], axis=1).astype(jnp.int32)
    spot_x = jnp.concatenate([obs[1:2, :], obs_far[1:2, :]], axis=1).astype(jnp.int32)
    one, zero = jnp.float32(1.0), jnp.float32(0.0)
    hot_x[...] = jnp.where(
        lax.broadcasted_iota(jnp.int32, (LON, 2 * SLOTS), 0) == spot_x, one, zero
    ).astype(jnp.bfloat16)
    hot = jnp.where(
        lax.broadcasted_iota(jnp.int32, (CELL_ROWS, 2 * SLOTS), 0) == spot_r, one, zero
    )
    hot_r[...] = hot.astype(jnp.bfloat16)
    parts = split(p[...].reshape(CELL_ROWS, LON))
    picked = dot(parts[0], hot_x[...]) + dot(parts[1], hot_x[...])
    read = jnp.sum(picked * hot, axis=0, keepdims=True)
    found[...] = read[:, SLOTS:]
    found_outer = misc(FOUND, found, found_far, win, outer)
    pl.when(inside)(lambda: found_outer.start())

    for mine in (0, 1):

        @pl.when(core == mine)
        def _():
            for dh in (1, 0):
                for there in (0, 1):
                    all_tiles(
                        lambda s: fwd(s, s, rows_of(mine)).wait_recv(), there, dh, dh == 0
                    )

    pl.when(inside)(lambda: found_outer.wait())
    depart[...] = jnp.where(
        obs[0:1, :] >= 0.0,
        precision[...] * (read[:, :SLOTS] + found_far[...] - innovation[...]),
        0.0,
    )
    depart_outer = misc(DEPART, depart, depart_far, win, outer)
    pl.when(inside)(lambda: depart_outer.start())

    def spec_wait(j):
        there_x, there_c = (xx + j // 2) % 4, (core + j % 2) % 2
        return copy(
            spec.at[there_x, :, there_c],
            spec.at[there_x, :, there_c],
            spec_s.at[j],
            spec_r.at[there_x * 2 + there_c],
            win,
            partner,
        )

    for j in range(1, 8):
        spec_wait(j).wait_recv()
    data = got[...].reshape(TILES, UNITS, EXT, 128)
    x = jnp.concatenate([data[:, u].reshape(TILES * EXT, 128) for u in range(UNITS)], axis=1)
    modal = dot3((ph[...], plo[...]), split(x))
    scale = spec[...].reshape(128, NLAT).T
    modal = modal * jnp.concatenate([scale] * UNITS, axis=1)
    back = dot3((qh[...], ql[...]), split(modal))
    for u in range(UNITS):
        unit = back[:, u * 128 : u * 128 + 128].reshape(TILES, EXT, 128)
        for t in range(TILES):
            send2[t * 40 + u * 8 : t * 40 + u * 8 + 8, :] = unit[t]

    for mine in (0, 1):

        @pl.when(core == mine)
        def _():
            for dh in (1, 0):
                for there in (0, 1):
                    all_tiles(
                        lambda d: bwd(d, me, rows_of(mine)).start(), there, dh, dh == 0
                    )

    got2[pl.ds(me * 40, 40), :] = send2[pl.ds(me * 40, 40), :]

    pl.when(inside)(lambda: depart_outer.wait())
    pushed = jnp.concatenate([depart[...], depart_far[...]], axis=1)
    high, low = split(hot_r[...].astype(jnp.float32) * pushed)
    force[...] = (dot_nt(high, hot_x[...]) + dot_nt(low, hot_x[...])).reshape(EXT, LEV, LON)

    for dh in (1, 0):
        for there in (0, 1):
            rows = rows_of(there)
            all_tiles(lambda s: bwd(s, s, rows).wait_recv(), there, dh, dh == 0)

    for i in range(EXT):
        for quarter in range(4):
            for b in range(9):
                lam[i, b * 8 : b * 8 + 8, quarter * 128 : quarter * 128 + 128] = got2[
                    pl.ds(unit_base(i, quarter, b), 8, stride=80), :
                ]
    passed = misc(LAMBDA, lam.at[pl.ds(0, ROWS)], lam_near, after, me)
    passed.start()

    table = (zh[...], zl[...])
    fields = dot3_nt(split(lam[...].reshape(CELL_ROWS, KEEP)), table).reshape(EXT, LEV, LON)
    force[...] = keep * fields - force[...]
    edge = misc(FORCE, force.at[pl.ds(0, 2)], force_near, win, partner)
    edge.start()
    edge.wait()

    def start(r):
        return force_near[-1 - r] if r < 0 else force[r]

    def back_step(get, r):
        cen, east, west = weights(la(r), lo(r), dr(r))
        mine = get(r)
        return (
            cen * mine
            + la(r + 1) * get(r + 1)
            + la(r - 1) * get(r - 1)
            + pltpu.roll(east * mine, 1, 1)
            + pltpu.roll(west * mine, LON - 1, 1)
        )

    for r in range(-1, ROWS + 1):
        mid[r + 1] = back_step(start, r)
    for r in range(ROWS):
        p[r] = back_step(lambda q: mid[q + 1], r)

    passed.wait()
    fields = dot3_nt(split(lam_near[...].reshape(ROWS * LEV, KEEP)), table)
    fields = fields.reshape(ROWS, LEV, LON)
    for i in range(ROWS):
        out[src(i)] = fields[i] - p[i]

    for there in (0, 1):
        rows = rows_of(there)
        for dh in (1, 0):
            all_tiles(lambda d: fwd(d, me, rows).wait_send(), there, dh, dh == 0)
    for mine in (0, 1):

        @pl.when(core == mine)
        def _():
            for dh in (1, 0):
                for there in (0, 1):
                    all_tiles(
                        lambda d: bwd(d, me, rows_of(mine)).wait_send(), there, dh, dh == 0
                    )

    for j in range(1, 8):
        spec_copy(j).wait_send()


def body(
    increment,
    background,
    lat_diffusion,
    lon_diffusion,
    advection,
    spectrum,
    obs_index,
    obs_count,
    innovation,
    obs_precision,
):
    zonal = two_parts(np.ascontiguousarray(zonal_table().T))
    merid = extended_meridional()
    merid_fwd = two_parts(merid)
    merid_back = two_parts(np.ascontiguousarray(merid.T))
    f32 = jnp.float32
    sems = pltpu.SemaphoreType.DMA
    scratch = [
        ((ROWS, LEV, KEEP), f32),
        ((ROWS, LEV, KEEP), f32),
        ((2, LEV, LON), f32),
        ((8, LON), f32),
        ((8, LON), f32),
        ((8, LON), f32),
        ((2, SLOTS), f32),
        ((2, SLOTS), f32),
        ((1, SLOTS), f32),
        ((1, SLOTS), f32),
        ((1, SLOTS), f32),
        ((1, SLOTS), f32),
        ((4, 2, 2, 8, NLAT), f32),
        ((EXT, LEV, LON), f32),
        ((EXT, LEV, LON), f32),
        ((EXT, LEV, KEEP), f32),
        ((TILES * 40, 128), f32),
        ((TILES * 40, 128), f32),
        ((LON, 2 * SLOTS), jnp.bfloat16),
        ((CELL_ROWS, 2 * SLOTS), jnp.bfloat16),
        ((EXT, LEV, KEEP), f32),
        ((ROWS, LEV, KEEP), f32),
        ((EXT, LEV, LON), f32),
        ((2, LEV, LON), f32),
    ]
    args = (
        increment[0].transpose(1, 0, 2),
        background.transpose(1, 0, 2),
        lat_diffusion[0],
        lon_diffusion[0],
        advection[0],
        spectrum,
        obs_index,
        obs_count,
        innovation,
        obs_precision,
        *zonal,
        *merid_fwd,
        *merid_back,
    )
    vmem = pl.BlockSpec(memory_space=pltpu.VMEM)
    gradient = pl.pallas_call(
        kernel,
        out_shape=jax.ShapeDtypeStruct((ROWS, LEV, LON), f32),
        in_specs=[vmem] * len(args),
        out_specs=vmem,
        scratch_shapes=[pltpu.VMEM(shape, kind) for shape, kind in scratch]
        + [sems((10,)), sems((10,)), sems((8,)), sems((8,))]
        + [sems((TILES,))] * 4
        + [pltpu.VMEM((TILES * 40, 128), f32)] * 2,
        compiler_params=pltpu.CompilerParams(
            vmem_limit_bytes=VMEM_LIMIT, collective_id=0, has_side_effects=True
        ),
    )(*args)
    return gradient.transpose(1, 0, 2)[None]


def solution(mesh):
    in_specs = (
        P("win", None, "tile", None),
        P(None, "tile", None),
        P("win", "tile", None),
        P("win", "tile", None),
        P("win", "tile", None),
        P("tile", None),
        P("win", "tile"),
        P("win", "tile"),
        P("win", "tile"),
        P("win", "tile"),
    )
    out_specs = P("win", None, "tile", None)
    return jax.shard_map(body, mesh=mesh, in_specs=in_specs, out_specs=out_specs, check_vma=False)
```

```python
import jax
import jax.numpy as jnp
import ml_dtypes
import numpy as np
from jax import lax
from jax.experimental import pallas as pl
from jax.experimental.pallas import tpu as pltpu
from jax.sharding import PartitionSpec as P

LEV, LON, ROWS, KEEP, NLAT, TILES, NWIN = 72, 768, 6, 512, 384, 64, 16
EXT = 8
VMEM_LIMIT = 58 * 1024 * 1024
SLOTS = 512
CELL_ROWS = EXT * LEV


def zonal_table():
    half = KEEP // 2
    wave = np.arange(KEEP)
    number = np.where(wave < half, wave, wave - half + 1)
    phase = number[:, None] * np.arange(LON)[None, :] % LON
    angle = 2.0 * np.pi * phase / LON
    scale = np.where(wave == 0, np.sqrt(1.0 / LON), np.sqrt(2.0 / LON))
    return np.where((wave < half)[:, None], np.cos(angle), np.sin(angle)) * scale[:, None]


def meridional_table():
    modes = np.arange(NLAT)
    phase = modes[:, None] * (2 * modes[None, :] + 1) % (4 * NLAT)
    scale = np.where(modes == 0, np.sqrt(1.0 / NLAT), np.sqrt(2.0 / NLAT))
    return np.cos(np.pi * phase / (2.0 * NLAT)) * scale[:, None]


def extended_meridional():
    table = meridional_table()
    out = np.zeros((NLAT, TILES, EXT))
    for tile in range(TILES):
        for i in range(EXT):
            row = tile * ROWS + (i if tile % 2 else ROWS - 1 - i)
            if 0 <= row < NLAT:
                out[:, tile, i] = table[:, row]
    return out.reshape(NLAT, TILES * EXT)


def two_parts(table):
    high = table.astype(ml_dtypes.bfloat16)
    low = (table - high.astype(np.float64)).astype(ml_dtypes.bfloat16)
    return high, low


def split(x):
    high = x.astype(jnp.bfloat16)
    low = (x - high.astype(jnp.float32)).astype(jnp.bfloat16)
    return high, low


def dot(a, b):
    return jnp.dot(a, b, preferred_element_type=jnp.float32)


def dot3(a, b):
    return dot(a[0], b[0]) + (dot(a[0], b[1]) + dot(a[1], b[0]))


def dot_nt(a, b):
    return lax.dot_general(a, b, (((1,), (1,)), ((), ())), preferred_element_type=jnp.float32)


def dot3_nt(a, b):
    return dot_nt(a[0], b[0]) + (dot_nt(a[0], b[1]) + dot_nt(a[1], b[0]))


def weights(a, b, c):
    return 1.0 - 2.0 * a - 2.0 * b, b - 0.5 * c, b + 0.5 * c


CHUNKS, DEEP = 3, LEV // 3
OWNER = (((0, 0), (0, 1), (1, 0)), ((0, 0), (1, 0), (1, 1)), ((0, 0), (0, 1), (1, 0)))
SPAN = 16
PART = TILES * SPAN


def unit_base(i, quarter, chunk, j):
    core, unit = OWNER[chunk][j]
    return chunk * PART + quarter * 16 * SPAN + core * SPAN + unit * 8 + i


def rows_of(chunk, core):
    return 8 * sum(owner == core for owner, _ in OWNER[chunk])


def rows_mixed(chunk, mine):
    return 32 * (rows_of(chunk, 0) + rows_of(chunk, 1)) - rows_of(chunk, mine)


HALO, PACK_IN, PACK_OUT, OBS, FOUND, DEPART, SPEC = range(7)
SHIFT, LAMBDA, FORCE = 7, 10, 13
MISC = 16


def kernel(
    inc,
    bg,
    lat,
    lon,
    drift,
    spectrum,
    cells,
    count,
    innovation,
    precision,
    zh,
    zl,
    ph,
    plo,
    qh,
    ql,
    out,
    coefs,
    shifted,
    near,
    pack,
    pack_in,
    pack_out,
    obs,
    obs_far,
    found,
    found_far,
    depart,
    depart_far,
    spec,
    p,
    mid,
    y,
    send,
    got,
    hot_x,
    hot_r,
    lam,
    lam_near,
    force,
    force_near,
    misc_s,
    misc_r,
    spec_s,
    spec_r,
    fwd_s,
    fwd_r,
    bwd_s,
    bwd_r,
    send2,
    got2,
):
    me = lax.axis_index("tile")
    win = lax.axis_index("win")
    core = me % 2
    half = (me // 2) % 2
    xx = (me // 4) % 4
    yy = me // 16
    inside = jnp.logical_and(me > 0, me < TILES - 1)
    partner = me + 1 - 2 * core
    outer = me + 2 * core - 1
    before = (win + NWIN - 1) % NWIN
    after = (win + 1) % NWIN

    def copy(src, dst, ssem, rsem, window, tile):
        return pltpu.make_async_remote_copy(
            src_ref=src,
            dst_ref=dst,
            send_sem=ssem,
            recv_sem=rsem,
            device_id=(window, tile),
            device_id_type=pl.DeviceIdType.MESH,
        )

    def misc(k, src, dst, window, tile):
        return copy(src, dst, misc_s.at[k], misc_r.at[k], window, tile)

    barrier = pltpu.get_barrier_semaphore()

    def greet(j, carry):
        pl.semaphore_signal(
            barrier,
            inc=1,
            device_id=(win, (me + j) % TILES),
            device_id_type=pl.DeviceIdType.MESH,
        )
        return carry

    for window in (before, after):
        pl.semaphore_signal(
            barrier, inc=1, device_id=(window, me), device_id_type=pl.DeviceIdType.MESH
        )
    lax.fori_loop(1, TILES, greet, 0)

    def src(i):
        return core * i + (1 - core) * (ROWS - 1 - i)

    pack[...] = jnp.zeros_like(pack)
    for k, (ref, i) in enumerate(
        ((lat, 0), (lat, 1), (lon, 0), (drift, 0), (lat, 5), (lat, 4), (lon, 5), (drift, 5))
    ):
        pack[k : k + 1, :] = ref[src(i)]
    spec[xx, half, core] = spectrum[...]

    number = cells[...].astype(jnp.float32)
    level = jnp.floor((number + 0.5) * (1.0 / (ROWS * LON)))
    rest = number - level * (ROWS * LON)
    row = jnp.floor((rest + 0.5) * (1.0 / LON))
    place = jnp.where(core == 0, ROWS - 1 - row, row)
    slot = lax.broadcasted_iota(jnp.int32, (1, SLOTS), 1)
    live = slot < count[...]
    obs[0:1, :] = jnp.where(live, place * LEV + level, -1.0)
    obs[1:2, :] = rest - row * LON

    @pl.when(jnp.logical_not(inside))
    def _():
        pack_out[...] = jnp.zeros_like(pack_out)
        obs_far[...] = jnp.zeros_like(obs_far)
        found_far[...] = jnp.zeros_like(found_far)
        depart_far[...] = jnp.zeros_like(depart_far)

    first = jnp.where(win == 0, 1.0, 0.0).astype(jnp.float32)
    table = (zh[...], zl[...])
    for n in range(CHUNKS):
        deep = pl.ds(n * DEEP, DEEP)
        field = inc[:, deep, :] - first * bg[:, deep, :]
        own = dot3(split(field.reshape(ROWS * DEEP, LON)), table).reshape(ROWS, DEEP, KEEP)
        for i in range(ROWS):
            coefs[n, src(i)] = own[i]

    pl.semaphore_wait(barrier, TILES + 1)

    shift = [misc(SHIFT + n, coefs.at[n], shifted.at[n], before, me) for n in range(CHUNKS)]
    pack_inner = misc(PACK_IN, pack, pack_in, win, partner)
    pack_outer = misc(PACK_OUT, pack, pack_out, win, outer)
    cells_outer = misc(OBS, obs, obs_far, win, outer)
    spec_across = misc(
        SPEC, spec.at[xx, half, core], spec.at[xx, half, core], win, me + 2 - 4 * half
    )
    rim = (1 - core) * (ROWS - 2)
    halo = misc(HALO, inc.at[pl.ds(rim, 2)], near, win, partner)
    pack_inner.start()
    halo.start()

    @pl.when(inside)
    def _():
        pack_outer.start()
        cells_outer.start()

    shift[0].start()
    spec_across.start()
    shift[1].start()
    shift[2].start()

    pack_inner.wait()
    halo.wait()

    @pl.when(inside)
    def _():
        pack_outer.wait()

    def la(r):
        if r < 0:
            return pack_in[-1 - r : -r, :]
        if r >= ROWS:
            return pack_out[r - 2 : r - 1, :]
        return lat[src(r)]

    def lo(r):
        if r < 0:
            return pack_in[2:3, :]
        if r >= ROWS:
            return pack_out[6:7, :]
        return lon[src(r)]

    def dr(r):
        if r < 0:
            return pack_in[3:4, :]
        if r >= ROWS:
            return pack_out[7:8, :]
        return drift[src(r)]

    def beyond(r):
        return near[core + (1 - 2 * core) * (-1 - r)]

    def state(r):
        return beyond(r) if r < 0 else inc[src(r)]

    def step(get, r, highest):
        a = la(r)
        if r > highest:
            return a * get(r - 1)
        cen, east, west = weights(a, lo(r), dr(r))
        mine = get(r)
        beside = get(r - 1)
        if r < highest:
            beside = beside + get(r + 1)
        return (
            cen * mine
            + a * beside
            + east * pltpu.roll(mine, LON - 1, 1)
            + west * pltpu.roll(mine, 1, 1)
        )

    for r in range(-1, ROWS + 1):
        mid[r + 1] = step(state, r, ROWS - 1)
    for r in range(EXT):
        p[r] = step(lambda q: mid[q + 1], r, ROWS)
    parts = split(p[...].reshape(CELL_ROWS, LON))
    y[...] = dot3(parts, table).reshape(EXT, LEV, KEEP)

    def spec_copy(j):
        return copy(
            spec.at[xx, :, core],
            spec.at[xx, :, core],
            spec_s.at[j],
            spec_r.at[xx * 2 + core],
            win,
            yy * 16 + (xx + j // 2) % 4 * 4 + half * 2 + (core + j % 2) % 2,
        )

    keep = jnp.where(win == NWIN - 1, 0.0, 1.0).astype(jnp.float32)

    def arrange(n):
        for i in range(EXT):
            c = -keep * y[i, n * DEEP : (n + 1) * DEEP, :]
            if i < ROWS:
                c = shifted[n, i] + c
            for quarter in range(4):
                for j in range(3):
                    send[pl.ds(unit_base(i, quarter, n, j), 8, stride=2 * SPAN), :] = c[
                        j * 8 : j * 8 + 8, quarter * 128 : quarter * 128 + 128
                    ]

    def block(ref, n, t, rows):
        return ref.at[pl.ds(n * PART + t * SPAN, rows), :]

    def fwd(n, d, rows):
        return copy(
            block(send, n, d, rows), block(got, n, me, rows), fwd_s.at[n], fwd_r.at[n], win, d
        )

    def bwd(n, d, rows):
        return copy(
            block(send2, n, d, rows), block(got2, n, me, rows), bwd_s.at[n], bwd_r.at[n], win, d
        )

    def total(ref, ref2, ssem, rsem, n, rows):
        whole = pl.ds(n * PART, rows)
        return copy(ref.at[whole, :], ref2.at[whole, :], ssem.at[n], rsem.at[n], win, partner)

    def all_tiles(act, dest_core, dh):
        def one(j, carry):
            d = (yy + j // 4) % 4 * 16 + (xx + j % 4) % 4 * 4 + (half + dh) % 2 * 2 + dest_core
            if dh == 0:
                pl.when(d != me)(lambda: act(d))
            else:
                act(d)
            return carry

        lax.fori_loop(0, 16, one, 0)

    def send_fwd(n):
        for dh in (1, 0):
            for there in (0, 1):
                all_tiles(lambda d: fwd(n, d, rows_of(n, there)).start(), there, dh)
        own_block = pl.ds(n * PART + me * SPAN, SPAN)
        got[own_block, :] = send[own_block, :]

    def send_bwd(n):
        for mine in (0, 1):

            @pl.when(core == mine)
            def _():
                for dh in (1, 0):
                    for there in (0, 1):
                        all_tiles(lambda d: bwd(n, d, rows_of(n, mine)).start(), there, dh)

        own_block = pl.ds(n * PART + me * SPAN, SPAN)
        got2[own_block, :] = send2[own_block, :]

    def by_core(act):
        for mine in (0, 1):
            pl.when(core == mine)(lambda: act(mine))

    def wait_fwd(n):
        by_core(
            lambda mine: total(
                send, got, fwd_s, fwd_r, n, (TILES - 1) * rows_of(n, mine)
            ).wait_recv()
        )

    def wait_bwd(n):
        by_core(
            lambda mine: total(send2, got2, bwd_s, bwd_r, n, rows_mixed(n, mine)).wait_recv()
        )

    shift[0].wait()
    arrange(0)
    send_fwd(0)

    spec_across.wait()
    for j in range(1, 8):
        spec_copy(j).start()

    @pl.when(inside)
    def _():
        cells_outer.wait()

    far_r = obs_far[0:1, :]
    far_r = jnp.where(
        far_r >= 5.0 * LEV, far_r + LEV, jnp.where(far_r >= 4.0 * LEV, far_r + 3.0 * LEV, -1.0)
    )
    one, zero = jnp.float32(1.0), jnp.float32(0.0)

    def hot(spots, size):
        spots = spots.astype(jnp.int32)
        numbers = lax.broadcasted_iota(jnp.int32, (size, SLOTS), 0)
        return jnp.where(numbers == spots, one, zero)

    def read(rows, longitudes, lanes):
        hot_x[:, lanes] = hot(longitudes, LON).astype(jnp.bfloat16)
        at = hot(rows, CELL_ROWS)
        hot_r[:, lanes] = at.astype(jnp.bfloat16)
        parts = split(p[...].reshape(CELL_ROWS, LON))
        picked = dot(parts[0], hot_x[:, lanes]) + dot(parts[1], hot_x[:, lanes])
        return jnp.sum(picked * at, axis=0, keepdims=True)

    found[...] = read(far_r, obs_far[1:2, :], slice(SLOTS, 2 * SLOTS))
    found_outer = misc(FOUND, found, found_far, win, outer)
    pl.when(inside)(lambda: found_outer.start())

    for n in (1, 2):
        shift[n].wait()
        arrange(n)
        send_fwd(n)

    depart[...] = read(obs[0:1, :], obs[1:2, :], slice(0, SLOTS))
    pl.when(inside)(lambda: found_outer.wait())
    depart[...] = jnp.where(
        obs[0:1, :] >= 0.0,
        precision[...] * (depart[...] + found_far[...] - innovation[...]),
        0.0,
    )
    depart_outer = misc(DEPART, depart, depart_far, win, outer)
    pl.when(inside)(lambda: depart_outer.start())

    def spec_wait(j):
        there_x, there_c = (xx + j // 2) % 4, (core + j % 2) % 2
        return copy(
            spec.at[there_x, :, there_c],
            spec.at[there_x, :, there_c],
            spec_s.at[j],
            spec_r.at[there_x * 2 + there_c],
            win,
            partner,
        )

    for j in range(1, 8):
        spec_wait(j).wait_recv()
    scale = spec[...].reshape(128, NLAT).T
    scale = jnp.concatenate([scale, scale], axis=1)
    for n in range(CHUNKS):
        wait_fwd(n)
        data = got[n * PART : (n + 1) * PART, :].reshape(TILES, 2, EXT, 128)
        x = jnp.concatenate([data[:, u].reshape(TILES * EXT, 128) for u in (0, 1)], axis=1)
        modal = dot3((ph[...], plo[...]), split(x)) * scale
        back = dot3((qh[...], ql[...]), split(modal))
        for u in (0, 1):
            unit = back[:, u * 128 : u * 128 + 128].reshape(TILES, EXT, 128)
            for t in range(TILES):
                at = n * PART + t * SPAN + u * 8
                send2[at : at + 8, :] = unit[t]
        send_bwd(n)
        if n == 1:
            pl.when(inside)(lambda: depart_outer.wait())
            pushed = jnp.concatenate([depart[...], depart_far[...]], axis=1)
            high, low = split(hot_r[...].astype(jnp.float32) * pushed)
            placed = dot_nt(high, hot_x[...]) + dot_nt(low, hot_x[...])
            force[...] = placed.reshape(EXT, LEV, LON)

    def back_step(get, r):
        cen, east, west = weights(la(r), lo(r), dr(r))
        mine = get(r)
        return (
            cen * mine
            + la(r + 1) * get(r + 1)
            + la(r - 1) * get(r - 1)
            + pltpu.roll(east * mine, 1, 1)
            + pltpu.roll(west * mine, LON - 1, 1)
        )

    passed = [
        misc(LAMBDA + n, lam.at[n, pl.ds(0, ROWS)], lam_near.at[n], after, me)
        for n in range(CHUNKS)
    ]
    edge = [
        misc(
            FORCE + n,
            force.at[pl.ds(0, 2), pl.ds(n * DEEP, DEEP), :],
            force_near.at[:, pl.ds(n * DEEP, DEEP), :],
            win,
            partner,
        )
        for n in range(CHUNKS)
    ]

    def receive(n):
        wait_bwd(n)
        for i in range(EXT):
            for quarter in range(4):
                for j in range(3):
                    lam[n, i, j * 8 : j * 8 + 8, quarter * 128 : quarter * 128 + 128] = got2[
                        pl.ds(unit_base(i, quarter, n, j), 8, stride=2 * SPAN), :
                    ]
        passed[n].start()
        fields = dot3_nt(split(lam[n].reshape(EXT * DEEP, KEEP)), (zh[...], zl[...]))
        fields = keep * fields.reshape(EXT, DEEP, LON)
        deep = pl.ds(n * DEEP, DEEP)
        force[:, deep, :] = fields - force[:, deep, :]
        edge[n].start()

    def adjoint(n):
        edge[n].wait()
        deep = pl.ds(n * DEEP, DEEP)

        def start(r):
            return force_near[-1 - r, deep, :] if r < 0 else force[r, deep, :]

        for r in range(-1, ROWS + 1):
            mid[r + 1, deep, :] = back_step(start, r)
        for r in range(ROWS):
            p[r, deep, :] = back_step(lambda q: mid[q + 1, deep, :], r)

    def finish(n):
        passed[n].wait()
        deep = pl.ds(n * DEEP, DEEP)
        fields = dot3_nt(split(lam_near[n].reshape(ROWS * DEEP, KEEP)), (zh[...], zl[...]))
        fields = fields.reshape(ROWS, DEEP, LON)
        for i in range(ROWS):
            out[src(i), deep, :] = fields[i] - p[i, deep, :]

    receive(0)
    adjoint(0)
    receive(1)
    adjoint(1)
    finish(0)
    receive(2)
    finish(1)
    adjoint(2)
    finish(2)

    for n in range(CHUNKS):
        by_core(
            lambda mine: total(send, got, fwd_s, fwd_r, n, rows_mixed(n, mine)).wait_send()
        )
        by_core(
            lambda mine: total(
                send2, got2, bwd_s, bwd_r, n, (TILES - 1) * rows_of(n, mine)
            ).wait_send()
        )
    for j in range(1, 8):
        spec_copy(j).wait_send()


def body(
    increment,
    background,
    lat_diffusion,
    lon_diffusion,
    advection,
    spectrum,
    obs_index,
    obs_count,
    innovation,
    obs_precision,
):
    zonal = two_parts(np.ascontiguousarray(zonal_table().T))
    merid = extended_meridional()
    merid_fwd = two_parts(merid)
    merid_back = two_parts(np.ascontiguousarray(merid.T))
    f32 = jnp.float32
    sems = pltpu.SemaphoreType.DMA
    scratch = [
        ((CHUNKS, ROWS, DEEP, KEEP), f32),
        ((CHUNKS, ROWS, DEEP, KEEP), f32),
        ((2, LEV, LON), f32),
        ((8, LON), f32),
        ((8, LON), f32),
        ((8, LON), f32),
        ((2, SLOTS), f32),
        ((2, SLOTS), f32),
        ((1, SLOTS), f32),
        ((1, SLOTS), f32),
        ((1, SLOTS), f32),
        ((1, SLOTS), f32),
        ((4, 2, 2, 8, NLAT), f32),
        ((EXT, LEV, LON), f32),
        ((EXT, LEV, LON), f32),
        ((EXT, LEV, KEEP), f32),
        ((CHUNKS * PART, 128), f32),
        ((CHUNKS * PART, 128), f32),
        ((LON, 2 * SLOTS), jnp.bfloat16),
        ((CELL_ROWS, 2 * SLOTS), jnp.bfloat16),
        ((CHUNKS, EXT, DEEP, KEEP), f32),
        ((CHUNKS, ROWS, DEEP, KEEP), f32),
        ((EXT, LEV, LON), f32),
        ((2, LEV, LON), f32),
    ]
    args = (
        increment[0].transpose(1, 0, 2),
        background.transpose(1, 0, 2),
        lat_diffusion.transpose(1, 0, 2),
        lon_diffusion.transpose(1, 0, 2),
        advection.transpose(1, 0, 2),
        spectrum,
        obs_index,
        obs_count,
        innovation,
        obs_precision,
        *zonal,
        *merid_fwd,
        *merid_back,
    )
    vmem = pl.BlockSpec(memory_space=pltpu.VMEM)
    gradient = pl.pallas_call(
        kernel,
        out_shape=jax.ShapeDtypeStruct((ROWS, LEV, LON), f32),
        in_specs=[vmem] * len(args),
        out_specs=vmem,
        scratch_shapes=[pltpu.VMEM(shape, kind) for shape, kind in scratch]
        + [sems((MISC,)), sems((MISC,)), sems((8,)), sems((8,))]
        + [sems((CHUNKS,))] * 4
        + [pltpu.VMEM((CHUNKS * PART, 128), f32)] * 2,
        compiler_params=pltpu.CompilerParams(
            vmem_limit_bytes=VMEM_LIMIT, collective_id=0, has_side_effects=True
        ),
    )(*args)
    return gradient.transpose(1, 0, 2)[None]


def solution(mesh):
    in_specs = (
        P("win", None, "tile", None),
        P(None, "tile", None),
        P("win", "tile", None),
        P("win", "tile", None),
        P("win", "tile", None),
        P("tile", None),
        P("win", "tile"),
        P("win", "tile"),
        P("win", "tile"),
        P("win", "tile"),
    )
    out_specs = P("win", None, "tile", None)
    return jax.shard_map(body, mesh=mesh, in_specs=in_specs, out_specs=out_specs, check_vma=False)
```

```python
import jax
import jax.numpy as jnp
import ml_dtypes
import numpy as np
from jax import lax
from jax.experimental import pallas as pl
from jax.experimental.pallas import tpu as pltpu
from jax.sharding import PartitionSpec as P

LEV, LON, ROWS, KEEP, NLAT, TILES, NWIN = 72, 768, 6, 512, 384, 64, 16
EXT = 8
VMEM_LIMIT = 58 * 1024 * 1024
SLOTS = 512
CELL_ROWS = EXT * LEV


def zonal_table():
    half = KEEP // 2
    wave = np.arange(KEEP)
    number = np.where(wave < half, wave, wave - half + 1)
    phase = number[:, None] * np.arange(LON)[None, :] % LON
    angle = 2.0 * np.pi * phase / LON
    scale = np.where(wave == 0, np.sqrt(1.0 / LON), np.sqrt(2.0 / LON))
    return np.where((wave < half)[:, None], np.cos(angle), np.sin(angle)) * scale[:, None]


def meridional_table():
    modes = np.arange(NLAT)
    phase = modes[:, None] * (2 * modes[None, :] + 1) % (4 * NLAT)
    scale = np.where(modes == 0, np.sqrt(1.0 / NLAT), np.sqrt(2.0 / NLAT))
    return np.cos(np.pi * phase / (2.0 * NLAT)) * scale[:, None]


def extended_meridional():
    table = meridional_table()
    out = np.zeros((NLAT, TILES, EXT))
    for tile in range(TILES):
        for i in range(EXT):
            row = tile * ROWS + (i if tile % 2 else ROWS - 1 - i)
            if 0 <= row < NLAT:
                out[:, tile, i] = table[:, row]
    return out.reshape(NLAT, TILES * EXT)


def two_parts(table):
    high = table.astype(ml_dtypes.bfloat16)
    low = (table - high.astype(np.float64)).astype(ml_dtypes.bfloat16)
    return high, low


def split(x):
    high = x.astype(jnp.bfloat16)
    low = (x - high.astype(jnp.float32)).astype(jnp.bfloat16)
    return high, low


def dot(a, b):
    return jnp.dot(a, b, preferred_element_type=jnp.float32)


def dot3(a, b):
    return dot(a[0], b[0]) + (dot(a[0], b[1]) + dot(a[1], b[0]))


def dot_nt(a, b):
    return lax.dot_general(a, b, (((1,), (1,)), ((), ())), preferred_element_type=jnp.float32)


def dot3_nt(a, b):
    return dot_nt(a[0], b[0]) + (dot_nt(a[0], b[1]) + dot_nt(a[1], b[0]))


def weights(a, b, c):
    return 1.0 - 2.0 * a - 2.0 * b, b - 0.5 * c, b + 0.5 * c


OWNER = (((0, 0), (1, 0)), ((0, 0), (0, 1), (0, 2), (1, 0), (1, 1)), ((0, 0), (1, 0)))
CHUNKS = len(OWNER)
DEEP = tuple(8 * len(owners) for owners in OWNER)
LEVEL0 = tuple(sum(DEEP[:n]) for n in range(CHUNKS))
WIDE = tuple(1 + max(unit for _, unit in owners) for owners in OWNER)
SPAN = tuple(8 * wide for wide in WIDE)
PART0 = tuple(TILES * sum(SPAN[:n]) for n in range(CHUNKS))
BLOCKS = TILES * sum(SPAN)


def unit_base(i, quarter, chunk, j):
    core, unit = OWNER[chunk][j]
    return PART0[chunk] + (quarter * 16 + core) * SPAN[chunk] + unit * 8 + i


def rows_of(chunk, core):
    return 8 * sum(owner == core for owner, _ in OWNER[chunk])


def rows_mixed(chunk, mine):
    return 32 * (rows_of(chunk, 0) + rows_of(chunk, 1)) - rows_of(chunk, mine)


HALO, PACK_IN, PACK_OUT, OBS, FOUND, DEPART, SPEC = range(7)
SHIFT, LAMBDA, FORCE = 7, 10, 13
MISC = 16


def kernel(
    inc,
    bg,
    lat,
    lon,
    drift,
    spectrum,
    cells,
    count,
    innovation,
    precision,
    zh,
    zl,
    ph,
    plo,
    qh,
    ql,
    out,
    coefs,
    shifted,
    near,
    pack,
    pack_in,
    pack_out,
    obs,
    obs_far,
    found,
    found_far,
    depart,
    depart_far,
    spec,
    p,
    mid,
    send,
    got,
    hot_x,
    hot_r,
    lam,
    lam_near,
    force,
    force_near,
    misc_s,
    misc_r,
    spec_s,
    spec_r,
    fwd_s,
    fwd_r,
    bwd_s,
    bwd_r,
    send2,
    got2,
):
    me = lax.axis_index("tile")
    win = lax.axis_index("win")
    core = me % 2
    half = (me // 2) % 2
    xx = (me // 4) % 4
    yy = me // 16
    inside = jnp.logical_and(me > 0, me < TILES - 1)
    partner = me + 1 - 2 * core
    outer = me + 2 * core - 1
    before = (win + NWIN - 1) % NWIN
    after = (win + 1) % NWIN

    def copy(src, dst, ssem, rsem, window, tile):
        return pltpu.make_async_remote_copy(
            src_ref=src,
            dst_ref=dst,
            send_sem=ssem,
            recv_sem=rsem,
            device_id=(window, tile),
            device_id_type=pl.DeviceIdType.MESH,
        )

    def misc(k, src, dst, window, tile):
        return copy(src, dst, misc_s.at[k], misc_r.at[k], window, tile)

    barrier = pltpu.get_barrier_semaphore()

    def greet(j, carry):
        pl.semaphore_signal(
            barrier,
            inc=1,
            device_id=(win, (me + j) % TILES),
            device_id_type=pl.DeviceIdType.MESH,
        )
        return carry

    for window in (before, after):
        pl.semaphore_signal(
            barrier, inc=1, device_id=(window, me), device_id_type=pl.DeviceIdType.MESH
        )
    lax.fori_loop(1, TILES, greet, 0)

    def src(i):
        return core * i + (1 - core) * (ROWS - 1 - i)

    pack[...] = jnp.zeros_like(pack)
    for k, (ref, i) in enumerate(
        ((lat, 0), (lat, 1), (lon, 0), (drift, 0), (lat, 5), (lat, 4), (lon, 5), (drift, 5))
    ):
        pack[k : k + 1, :] = ref[src(i)]
    spec[xx, half, core] = spectrum[...]

    number = cells[...].astype(jnp.float32)
    level = jnp.floor((number + 0.5) * (1.0 / (ROWS * LON)))
    rest = number - level * (ROWS * LON)
    row = jnp.floor((rest + 0.5) * (1.0 / LON))
    place = jnp.where(core == 0, ROWS - 1 - row, row)
    slot = lax.broadcasted_iota(jnp.int32, (1, SLOTS), 1)
    live = slot < count[...]
    obs[0:1, :] = jnp.where(live, place * LEV + level, -1.0)
    obs[1:2, :] = rest - row * LON

    @pl.when(jnp.logical_not(inside))
    def _():
        pack_out[...] = jnp.zeros_like(pack_out)
        obs_far[...] = jnp.zeros_like(obs_far)
        found_far[...] = jnp.zeros_like(found_far)
        depart_far[...] = jnp.zeros_like(depart_far)

    first = jnp.where(win == 0, 1.0, 0.0).astype(jnp.float32)
    table = (zh[...], zl[...])
    for n in range(CHUNKS):
        deep = pl.ds(LEVEL0[n], DEEP[n])
        field = inc[:, deep, :] - first * bg[:, deep, :]
        own = dot3(split(field.reshape(ROWS * DEEP[n], LON)), table)
        own = own.reshape(ROWS, DEEP[n], KEEP)
        for i in range(ROWS):
            coefs[pl.ds(ROWS * LEVEL0[n] + src(i) * DEEP[n], DEEP[n]), :] = own[i]

    pl.semaphore_wait(barrier, TILES + 1)

    def six(ref, n):
        return ref.at[pl.ds(ROWS * LEVEL0[n], ROWS * DEEP[n]), :]

    shift = [
        misc(SHIFT + n, six(coefs, n), six(shifted, n), before, me) for n in range(CHUNKS)
    ]
    pack_inner = misc(PACK_IN, pack, pack_in, win, partner)
    pack_outer = misc(PACK_OUT, pack, pack_out, win, outer)
    cells_outer = misc(OBS, obs, obs_far, win, outer)
    spec_across = misc(
        SPEC, spec.at[xx, half, core], spec.at[xx, half, core], win, me + 2 - 4 * half
    )
    rim = (1 - core) * (ROWS - 2)
    halo = misc(HALO, inc.at[pl.ds(rim, 2)], near, win, partner)
    pack_inner.start()
    halo.start()

    @pl.when(inside)
    def _():
        pack_outer.start()
        cells_outer.start()

    shift[0].start()
    spec_across.start()
    shift[1].start()
    shift[2].start()

    pack_inner.wait()
    halo.wait()

    @pl.when(inside)
    def _():
        pack_outer.wait()

    def la(r):
        if r < 0:
            return pack_in[-1 - r : -r, :]
        if r >= ROWS:
            return pack_out[r - 2 : r - 1, :]
        return lat[src(r)]

    def lo(r):
        if r < 0:
            return pack_in[2:3, :]
        if r >= ROWS:
            return pack_out[6:7, :]
        return lon[src(r)]

    def dr(r):
        if r < 0:
            return pack_in[3:4, :]
        if r >= ROWS:
            return pack_out[7:8, :]
        return drift[src(r)]

    def beyond(r):
        return near[core + (1 - 2 * core) * (-1 - r)]

    def state(r):
        return beyond(r) if r < 0 else inc[src(r)]

    def step(get, r, highest):
        a = la(r)
        if r > highest:
            return a * get(r - 1)
        cen, east, west = weights(a, lo(r), dr(r))
        mine = get(r)
        beside = get(r - 1)
        if r < highest:
            beside = beside + get(r + 1)
        return (
            cen * mine
            + a * beside
            + east * pltpu.roll(mine, LON - 1, 1)
            + west * pltpu.roll(mine, 1, 1)
        )

    for r in range(-1, ROWS + 1):
        mid[r + 1] = step(state, r, ROWS - 1)
    for r in range(EXT):
        p[r] = step(lambda q: mid[q + 1], r, ROWS)
    def spec_copy(j):
        return copy(
            spec.at[xx, :, core],
            spec.at[xx, :, core],
            spec_s.at[j],
            spec_r.at[xx * 2 + core],
            win,
            yy * 16 + (xx + j // 2) % 4 * 4 + half * 2 + (core + j % 2) % 2,
        )

    keep = jnp.where(win == NWIN - 1, 0.0, 1.0).astype(jnp.float32)

    def arrange(n):
        rows = p[:, LEVEL0[n] : LEVEL0[n] + DEEP[n], :].reshape(EXT * DEEP[n], LON)
        y = dot3(split(rows), (zh[...], zl[...])).reshape(EXT, DEEP[n], KEEP)
        shift[n].wait()
        for i in range(EXT):
            c = -keep * y[i]
            if i < ROWS:
                at = ROWS * LEVEL0[n] + i * DEEP[n]
                c = shifted[at : at + DEEP[n], :] + c
            for quarter in range(4):
                for j in range(len(OWNER[n])):
                    send[pl.ds(unit_base(i, quarter, n, j), 8, stride=2 * SPAN[n]), :] = c[
                        j * 8 : j * 8 + 8, quarter * 128 : quarter * 128 + 128
                    ]

    def block(ref, n, t, rows):
        return ref.at[pl.ds(PART0[n] + t * SPAN[n], rows), :]

    def fwd(n, d, rows):
        return copy(
            block(send, n, d, rows), block(got, n, me, rows), fwd_s.at[n], fwd_r.at[n], win, d
        )

    def bwd(n, d, rows):
        return copy(
            block(send2, n, d, rows), block(got2, n, me, rows), bwd_s.at[n], bwd_r.at[n], win, d
        )

    def total(ref, ref2, ssem, rsem, n, rows):
        whole = pl.ds(PART0[n], rows)
        return copy(ref.at[whole, :], ref2.at[whole, :], ssem.at[n], rsem.at[n], win, partner)

    def all_tiles(act, there):
        def one(j, carry):
            chip = (yy + j // 4) % 4 * 16 + (xx + j % 4) % 4 * 4 + there
            act(chip + (1 - half) * 2)
            close = chip + half * 2
            pl.when(close != me)(lambda: act(close))
            return carry

        lax.fori_loop(0, 16, one, 0)

    def own_block(n):
        return pl.ds(PART0[n] + me * SPAN[n], SPAN[n])

    def send_fwd(n):
        for there in (0, 1):
            all_tiles(lambda d: fwd(n, d, rows_of(n, there)).start(), there)
        got[own_block(n), :] = send[own_block(n), :]

    def send_bwd(n):
        for mine in (0, 1):

            @pl.when(core == mine)
            def _():
                for there in (0, 1):
                    all_tiles(lambda d: bwd(n, d, rows_of(n, mine)).start(), there)

        got2[own_block(n), :] = send2[own_block(n), :]

    def by_core(act):
        for mine in (0, 1):
            pl.when(core == mine)(lambda: act(mine))

    def wait_fwd(n):
        by_core(
            lambda mine: total(
                send, got, fwd_s, fwd_r, n, (TILES - 1) * rows_of(n, mine)
            ).wait_recv()
        )

    def wait_bwd(n):
        by_core(
            lambda mine: total(send2, got2, bwd_s, bwd_r, n, rows_mixed(n, mine)).wait_recv()
        )

    arrange(0)
    send_fwd(0)

    spec_across.wait()
    for j in range(1, 8):
        spec_copy(j).start()

    @pl.when(inside)
    def _():
        cells_outer.wait()

    far_r = obs_far[0:1, :]
    far_r = jnp.where(
        far_r >= 5.0 * LEV, far_r + LEV, jnp.where(far_r >= 4.0 * LEV, far_r + 3.0 * LEV, -1.0)
    )
    one, zero = jnp.float32(1.0), jnp.float32(0.0)

    def hot(spots, size):
        spots = spots.astype(jnp.int32)
        numbers = lax.broadcasted_iota(jnp.int32, (size, SLOTS), 0)
        return jnp.where(numbers == spots, one, zero)

    def read(rows, longitudes, lanes):
        hot_x[:, lanes] = hot(longitudes, LON).astype(jnp.bfloat16)
        at = hot(rows, CELL_ROWS)
        hot_r[:, lanes] = at.astype(jnp.bfloat16)
        parts = split(p[...].reshape(CELL_ROWS, LON))
        picked = dot(parts[0], hot_x[:, lanes]) + dot(parts[1], hot_x[:, lanes])
        return jnp.sum(picked * at, axis=0, keepdims=True)

    found[...] = read(far_r, obs_far[1:2, :], slice(SLOTS, 2 * SLOTS))
    found_outer = misc(FOUND, found, found_far, win, outer)
    pl.when(inside)(lambda: found_outer.start())

    for n in (1, 2):
        arrange(n)
        send_fwd(n)

    depart[...] = read(obs[0:1, :], obs[1:2, :], slice(0, SLOTS))
    pl.when(inside)(lambda: found_outer.wait())
    depart[...] = jnp.where(
        obs[0:1, :] >= 0.0,
        precision[...] * (depart[...] + found_far[...] - innovation[...]),
        0.0,
    )
    depart_outer = misc(DEPART, depart, depart_far, win, outer)
    pl.when(inside)(lambda: depart_outer.start())

    def spec_wait(j):
        there_x, there_c = (xx + j // 2) % 4, (core + j % 2) % 2
        return copy(
            spec.at[there_x, :, there_c],
            spec.at[there_x, :, there_c],
            spec_s.at[j],
            spec_r.at[there_x * 2 + there_c],
            win,
            partner,
        )

    for j in range(1, 8):
        spec_wait(j).wait_recv()
    scale = spec[...].reshape(128, NLAT).T
    for n in range(CHUNKS):
        wait_fwd(n)
        units = range(WIDE[n])
        data = got[PART0[n] : PART0[n] + TILES * SPAN[n], :]
        data = data.reshape(TILES, WIDE[n], EXT, 128)
        x = jnp.concatenate([data[:, u].reshape(TILES * EXT, 128) for u in units], axis=1)
        modal = dot3((ph[...], plo[...]), split(x))
        modal = modal * jnp.concatenate([scale] * WIDE[n], axis=1)
        back = dot3((qh[...], ql[...]), split(modal))
        for u in units:
            unit = back[:, u * 128 : u * 128 + 128].reshape(TILES, EXT, 128)
            for t in range(TILES):
                at = PART0[n] + t * SPAN[n] + u * 8
                send2[at : at + 8, :] = unit[t]
        send_bwd(n)
        if n == 1:
            pl.when(inside)(lambda: depart_outer.wait())
            pushed = jnp.concatenate([depart[...], depart_far[...]], axis=1)
            high, low = split(hot_r[...].astype(jnp.float32) * pushed)
            placed = dot_nt(high, hot_x[...]) + dot_nt(low, hot_x[...])
            force[...] = placed.reshape(EXT, LEV, LON)

    def back_step(get, r):
        cen, east, west = weights(la(r), lo(r), dr(r))
        mine = get(r)
        return (
            cen * mine
            + la(r + 1) * get(r + 1)
            + la(r - 1) * get(r - 1)
            + pltpu.roll(east * mine, 1, 1)
            + pltpu.roll(west * mine, LON - 1, 1)
        )

    passed = [
        misc(
            LAMBDA + n,
            lam.at[pl.ds(EXT * LEVEL0[n], ROWS * DEEP[n]), :],
            six(lam_near, n),
            after,
            me,
        )
        for n in range(CHUNKS)
    ]
    edge = [
        misc(
            FORCE + n,
            force.at[pl.ds(0, 2), pl.ds(LEVEL0[n], DEEP[n]), :],
            force_near.at[:, pl.ds(LEVEL0[n], DEEP[n]), :],
            win,
            partner,
        )
        for n in range(CHUNKS)
    ]

    def receive(n):
        wait_bwd(n)
        for i in range(EXT):
            for quarter in range(4):
                for j in range(len(OWNER[n])):
                    at = EXT * LEVEL0[n] + i * DEEP[n] + j * 8
                    lam[at : at + 8, quarter * 128 : quarter * 128 + 128] = got2[
                        pl.ds(unit_base(i, quarter, n, j), 8, stride=2 * SPAN[n]), :
                    ]
        passed[n].start()
        rows = lam[EXT * LEVEL0[n] : EXT * (LEVEL0[n] + DEEP[n]), :]
        fields = dot3_nt(split(rows), (zh[...], zl[...]))
        fields = keep * fields.reshape(EXT, DEEP[n], LON)
        deep = pl.ds(LEVEL0[n], DEEP[n])
        force[:, deep, :] = fields - force[:, deep, :]
        edge[n].start()

    def adjoint(n):
        edge[n].wait()
        deep = pl.ds(LEVEL0[n], DEEP[n])

        def start(r):
            return force_near[-1 - r, deep, :] if r < 0 else force[r, deep, :]

        for r in range(-1, ROWS + 1):
            mid[r + 1, deep, :] = back_step(start, r)
        for r in range(ROWS):
            p[r, deep, :] = back_step(lambda q: mid[q + 1, deep, :], r)

    def finish(n):
        passed[n].wait()
        deep = pl.ds(LEVEL0[n], DEEP[n])
        rows = lam_near[ROWS * LEVEL0[n] : ROWS * (LEVEL0[n] + DEEP[n]), :]
        fields = dot3_nt(split(rows), (zh[...], zl[...])).reshape(ROWS, DEEP[n], LON)
        for i in range(ROWS):
            out[src(i), deep, :] = fields[i] - p[i, deep, :]

    receive(0)
    adjoint(0)
    receive(1)
    adjoint(1)
    finish(0)
    receive(2)
    finish(1)
    adjoint(2)
    finish(2)

    for n in range(CHUNKS):
        by_core(
            lambda mine: total(send, got, fwd_s, fwd_r, n, rows_mixed(n, mine)).wait_send()
        )
        by_core(
            lambda mine: total(
                send2, got2, bwd_s, bwd_r, n, (TILES - 1) * rows_of(n, mine)
            ).wait_send()
        )
    for j in range(1, 8):
        spec_copy(j).wait_send()


def body(
    increment,
    background,
    lat_diffusion,
    lon_diffusion,
    advection,
    spectrum,
    obs_index,
    obs_count,
    innovation,
    obs_precision,
):
    zonal = two_parts(np.ascontiguousarray(zonal_table().T))
    merid = extended_meridional()
    merid_fwd = two_parts(merid)
    merid_back = two_parts(np.ascontiguousarray(merid.T))
    f32 = jnp.float32
    sems = pltpu.SemaphoreType.DMA
    scratch = [
        ((ROWS * LEV, KEEP), f32),
        ((ROWS * LEV, KEEP), f32),
        ((2, LEV, LON), f32),
        ((8, LON), f32),
        ((8, LON), f32),
        ((8, LON), f32),
        ((2, SLOTS), f32),
        ((2, SLOTS), f32),
        ((1, SLOTS), f32),
        ((1, SLOTS), f32),
        ((1, SLOTS), f32),
        ((1, SLOTS), f32),
        ((4, 2, 2, 8, NLAT), f32),
        ((EXT, LEV, LON), f32),
        ((EXT, LEV, LON), f32),
        ((BLOCKS, 128), f32),
        ((BLOCKS, 128), f32),
        ((LON, 2 * SLOTS), jnp.bfloat16),
        ((CELL_ROWS, 2 * SLOTS), jnp.bfloat16),
        ((EXT * LEV, KEEP), f32),
        ((ROWS * LEV, KEEP), f32),
        ((EXT, LEV, LON), f32),
        ((2, LEV, LON), f32),
    ]
    args = (
        increment[0].transpose(1, 0, 2),
        background.transpose(1, 0, 2),
        lat_diffusion.transpose(1, 0, 2),
        lon_diffusion.transpose(1, 0, 2),
        advection.transpose(1, 0, 2),
        spectrum,
        obs_index,
        obs_count,
        innovation,
        obs_precision,
        *zonal,
        *merid_fwd,
        *merid_back,
    )
    vmem = pl.BlockSpec(memory_space=pltpu.VMEM)
    gradient = pl.pallas_call(
        kernel,
        out_shape=jax.ShapeDtypeStruct((ROWS, LEV, LON), f32),
        in_specs=[vmem] * len(args),
        out_specs=vmem,
        scratch_shapes=[pltpu.VMEM(shape, kind) for shape, kind in scratch]
        + [sems((MISC,)), sems((MISC,)), sems((8,)), sems((8,))]
        + [sems((CHUNKS,))] * 4
        + [pltpu.VMEM((BLOCKS, 128), f32)] * 2,
        compiler_params=pltpu.CompilerParams(
            vmem_limit_bytes=VMEM_LIMIT, collective_id=0, has_side_effects=True
        ),
    )(*args)
    return gradient.transpose(1, 0, 2)[None]


def solution(mesh):
    in_specs = (
        P("win", None, "tile", None),
        P(None, "tile", None),
        P("win", "tile", None),
        P("win", "tile", None),
        P("win", "tile", None),
        P("tile", None),
        P("win", "tile"),
        P("win", "tile"),
        P("win", "tile"),
        P("win", "tile"),
    )
    out_specs = P("win", None, "tile", None)
    return jax.shard_map(body, mesh=mesh, in_specs=in_specs, out_specs=out_specs, check_vma=False)
```

```python
import jax
import jax.numpy as jnp
import ml_dtypes
import numpy as np
from jax import lax
from jax.experimental import pallas as pl
from jax.experimental.pallas import tpu as pltpu
from jax.sharding import PartitionSpec as P

LEV, LON, ROWS, KEEP, NLAT, TILES, NWIN = 72, 768, 6, 512, 384, 64, 16
EXT = 8
VMEM_LIMIT = 58 * 1024 * 1024
SLOTS = 512
CELL_ROWS = EXT * LEV


def zonal_table():
    half = KEEP // 2
    wave = np.arange(KEEP)
    number = np.where(wave < half, wave, wave - half + 1)
    phase = number[:, None] * np.arange(LON)[None, :] % LON
    angle = 2.0 * np.pi * phase / LON
    scale = np.where(wave == 0, np.sqrt(1.0 / LON), np.sqrt(2.0 / LON))
    return np.where((wave < half)[:, None], np.cos(angle), np.sin(angle)) * scale[:, None]


def meridional_table():
    modes = np.arange(NLAT)
    phase = modes[:, None] * (2 * modes[None, :] + 1) % (4 * NLAT)
    scale = np.where(modes == 0, np.sqrt(1.0 / NLAT), np.sqrt(2.0 / NLAT))
    return np.cos(np.pi * phase / (2.0 * NLAT)) * scale[:, None]


def extended_meridional():
    table = meridional_table()
    out = np.zeros((NLAT, TILES, EXT))
    for tile in range(TILES):
        for i in range(EXT):
            row = tile * ROWS + (i if tile % 2 else ROWS - 1 - i)
            if 0 <= row < NLAT:
                out[:, tile, i] = table[:, row]
    return out.reshape(NLAT, TILES * EXT)


def two_parts(table):
    high = table.astype(ml_dtypes.bfloat16)
    low = (table - high.astype(np.float64)).astype(ml_dtypes.bfloat16)
    return high, low


def split(x):
    high = x.astype(jnp.bfloat16)
    low = (x - high.astype(jnp.float32)).astype(jnp.bfloat16)
    return high, low


def dot(a, b):
    return jnp.dot(a, b, preferred_element_type=jnp.float32)


def dot3(a, b):
    return dot(a[0], b[0]) + (dot(a[0], b[1]) + dot(a[1], b[0]))


def dot_nt(a, b):
    return lax.dot_general(a, b, (((1,), (1,)), ((), ())), preferred_element_type=jnp.float32)


def dot3_nt(a, b):
    return dot_nt(a[0], b[0]) + (dot_nt(a[0], b[1]) + dot_nt(a[1], b[0]))


def weights(a, b, c):
    return 1.0 - 2.0 * a - 2.0 * b, b - 0.5 * c, b + 0.5 * c


OWNER = (((0, 0), (1, 0)), ((0, 0), (0, 1), (0, 2), (1, 0), (1, 1)), ((0, 0), (1, 0)))
CHUNKS = len(OWNER)
DEEP = tuple(8 * len(owners) for owners in OWNER)
LEVEL0 = tuple(sum(DEEP[:n]) for n in range(CHUNKS))
WIDE = tuple(1 + max(unit for _, unit in owners) for owners in OWNER)
SPAN = tuple(8 * wide for wide in WIDE)
PART0 = tuple(TILES * sum(SPAN[:n]) for n in range(CHUNKS))
BLOCKS = TILES * sum(SPAN)


def unit_base(i, quarter, chunk, j):
    core, unit = OWNER[chunk][j]
    return PART0[chunk] + (quarter * 16 + core) * SPAN[chunk] + unit * 8 + i


def rows_of(chunk, core):
    return 8 * sum(owner == core for owner, _ in OWNER[chunk])


def rows_mixed(chunk, mine):
    return 32 * (rows_of(chunk, 0) + rows_of(chunk, 1)) - rows_of(chunk, mine)


HALO, PACK_IN, PACK_OUT, OBS, FOUND, DEPART, SPEC = range(7)
SHIFT, LAMBDA, FORCE = 7, 10, 13
MISC = 16


def kernel(
    inc,
    bg,
    lat,
    lon,
    drift,
    spectrum,
    cells,
    count,
    innovation,
    precision,
    zh,
    zl,
    ph,
    plo,
    qh,
    ql,
    out,
    coefs,
    shifted,
    near,
    pack,
    pack_in,
    pack_out,
    obs,
    obs_far,
    found,
    found_far,
    depart,
    depart_far,
    spec,
    p,
    mid,
    send,
    got,
    hot_x,
    hot_r,
    lam,
    lam_near,
    force,
    force_near,
    misc_s,
    misc_r,
    spec_s,
    spec_r,
    fwd_s,
    fwd_r,
    bwd_s,
    bwd_r,
    send2,
    got2,
):
    me = lax.axis_index("tile")
    win = lax.axis_index("win")
    core = me % 2
    half = (me // 2) % 2
    xx = (me // 4) % 4
    yy = me // 16
    inside = jnp.logical_and(me > 0, me < TILES - 1)
    partner = me + 1 - 2 * core
    outer = me + 2 * core - 1
    before = (win + NWIN - 1) % NWIN
    after = (win + 1) % NWIN
    is_first, is_last = 1 - (win + NWIN - 1) // NWIN, (win + 1) // NWIN
    mirror = me + 2 - 4 * half
    before_tile = me + is_first * (2 - 4 * half)
    after_tile = me + is_last * (2 - 4 * half)

    def rows_at(t):
        return t + is_last * (2 - 4 * ((t // 2) % 2))

    def copy(src, dst, ssem, rsem, window, tile):
        return pltpu.make_async_remote_copy(
            src_ref=src,
            dst_ref=dst,
            send_sem=ssem,
            recv_sem=rsem,
            device_id=(window, tile),
            device_id_type=pl.DeviceIdType.MESH,
        )

    def misc(k, src, dst, window, tile):
        return copy(src, dst, misc_s.at[k], misc_r.at[k], window, tile)

    barrier = pltpu.get_barrier_semaphore()

    def greet(j, carry):
        pl.semaphore_signal(
            barrier,
            inc=1,
            device_id=(win, (me + j) % TILES),
            device_id_type=pl.DeviceIdType.MESH,
        )
        return carry

    for neighbour in ((before, before_tile), (after, after_tile)):
        pl.semaphore_signal(
            barrier, inc=1, device_id=neighbour, device_id_type=pl.DeviceIdType.MESH
        )
    lax.fori_loop(1, TILES, greet, 0)

    def src(i):
        return core * i + (1 - core) * (ROWS - 1 - i)

    pack[...] = jnp.zeros_like(pack)
    for k, (ref, i) in enumerate(
        ((lat, 0), (lat, 1), (lon, 0), (drift, 0), (lat, 5), (lat, 4), (lon, 5), (drift, 5))
    ):
        pack[k : k + 1, :] = ref[src(i)]
    spec[xx, half, core] = spectrum[...]

    number = cells[...].astype(jnp.float32)
    level = jnp.floor((number + 0.5) * (1.0 / (ROWS * LON)))
    rest = number - level * (ROWS * LON)
    row = jnp.floor((rest + 0.5) * (1.0 / LON))
    place = jnp.where(core == 0, ROWS - 1 - row, row)
    slot = lax.broadcasted_iota(jnp.int32, (1, SLOTS), 1)
    live = slot < count[...]
    obs[0:1, :] = jnp.where(live, place * LEV + level, -1.0)
    obs[1:2, :] = rest - row * LON

    @pl.when(jnp.logical_not(inside))
    def _():
        pack_out[...] = jnp.zeros_like(pack_out)
        obs_far[...] = jnp.zeros_like(obs_far)
        found_far[...] = jnp.zeros_like(found_far)
        depart_far[...] = jnp.zeros_like(depart_far)

    first = jnp.where(win == 0, 1.0, 0.0).astype(jnp.float32)
    table = (zh[...], zl[...])
    for n in range(CHUNKS):
        deep = pl.ds(LEVEL0[n], DEEP[n])
        field = inc[:, deep, :] - first * bg[:, deep, :]
        own = dot3(split(field.reshape(ROWS * DEEP[n], LON)), table)
        own = own.reshape(ROWS, DEEP[n], KEEP)
        for i in range(ROWS):
            coefs[pl.ds(ROWS * LEVEL0[n] + src(i) * DEEP[n], DEEP[n]), :] = own[i]

    pl.semaphore_wait(barrier, TILES + 1)

    def six(ref, n):
        return ref.at[pl.ds(ROWS * LEVEL0[n], ROWS * DEEP[n]), :]

    shift = [
        misc(SHIFT + n, six(coefs, n), six(shifted, n), before, before_tile) for n in range(CHUNKS)
    ]
    pack_inner = misc(PACK_IN, pack, pack_in, win, partner)
    pack_outer = misc(PACK_OUT, pack, pack_out, win, outer)
    cells_outer = misc(OBS, obs, obs_far, win, outer)
    spec_across = misc(
        SPEC, spec.at[xx, half, core], spec.at[xx, half, core], win, mirror
    )
    rim = (1 - core) * (ROWS - 2)
    halo = misc(HALO, inc.at[pl.ds(rim, 2)], near, win, partner)
    pack_inner.start()
    halo.start()

    @pl.when(inside)
    def _():
        pack_outer.start()
        cells_outer.start()

    shift[0].start()
    spec_across.start()
    shift[1].start()
    shift[2].start()

    pack_inner.wait()
    halo.wait()

    @pl.when(inside)
    def _():
        pack_outer.wait()

    def la(r):
        if r < 0:
            return pack_in[-1 - r : -r, :]
        if r >= ROWS:
            return pack_out[r - 2 : r - 1, :]
        return lat[src(r)]

    def lo(r):
        if r < 0:
            return pack_in[2:3, :]
        if r >= ROWS:
            return pack_out[6:7, :]
        return lon[src(r)]

    def dr(r):
        if r < 0:
            return pack_in[3:4, :]
        if r >= ROWS:
            return pack_out[7:8, :]
        return drift[src(r)]

    def beyond(r):
        return near[core + (1 - 2 * core) * (-1 - r)]

    def state(r):
        return beyond(r) if r < 0 else inc[src(r)]

    def step(get, r, highest):
        a = la(r)
        if r > highest:
            return a * get(r - 1)
        cen, east, west = weights(a, lo(r), dr(r))
        mine = get(r)
        beside = get(r - 1)
        if r < highest:
            beside = beside + get(r + 1)
        return (
            cen * mine
            + a * beside
            + east * pltpu.roll(mine, LON - 1, 1)
            + west * pltpu.roll(mine, 1, 1)
        )

    for r in range(-1, ROWS + 1):
        mid[r + 1] = step(state, r, ROWS - 1)
    for r in range(EXT):
        p[r] = step(lambda q: mid[q + 1], r, ROWS)
    def spec_copy(j):
        return copy(
            spec.at[xx, :, core],
            spec.at[xx, :, core],
            spec_s.at[j],
            spec_r.at[xx * 2 + core],
            win,
            yy * 16 + (xx + j // 2) % 4 * 4 + half * 2 + (core + j % 2) % 2,
        )

    keep = jnp.where(win == NWIN - 1, 0.0, 1.0).astype(jnp.float32)

    def arrange(n):
        rows = p[:, LEVEL0[n] : LEVEL0[n] + DEEP[n], :].reshape(EXT * DEEP[n], LON)
        y = dot3(split(rows), (zh[...], zl[...])).reshape(EXT, DEEP[n], KEEP)
        shift[n].wait()
        for i in range(EXT):
            c = -keep * y[i]
            if i < ROWS:
                at = ROWS * LEVEL0[n] + i * DEEP[n]
                c = shifted[at : at + DEEP[n], :] + c
            for quarter in range(4):
                for j in range(len(OWNER[n])):
                    send[pl.ds(unit_base(i, quarter, n, j), 8, stride=2 * SPAN[n]), :] = c[
                        j * 8 : j * 8 + 8, quarter * 128 : quarter * 128 + 128
                    ]

    def block(ref, n, t, rows):
        return ref.at[pl.ds(PART0[n] + t * SPAN[n], rows), :]

    def fwd(n, d, rows):
        return copy(
            block(send, n, d, rows), block(got, n, rows_at(me), rows), fwd_s.at[n], fwd_r.at[n], win, d
        )

    def bwd(n, d, rows):
        return copy(
            block(send2, n, rows_at(d), rows), block(got2, n, me, rows), bwd_s.at[n], bwd_r.at[n], win, d
        )

    def total(ref, ref2, ssem, rsem, n, rows):
        whole = pl.ds(PART0[n], rows)
        return copy(ref.at[whole, :], ref2.at[whole, :], ssem.at[n], rsem.at[n], win, partner)

    def all_tiles(act, there):
        def one(j, carry):
            chip = (yy + j // 4) % 4 * 16 + (xx + j % 4) % 4 * 4 + there
            act(chip + (1 - half) * 2)
            close = chip + half * 2
            pl.when(close != me)(lambda: act(close))
            return carry

        lax.fori_loop(0, 16, one, 0)

    def own_block(n, t):
        return pl.ds(PART0[n] + t * SPAN[n], SPAN[n])

    def send_fwd(n):
        for there in (0, 1):
            all_tiles(lambda d: fwd(n, d, rows_of(n, there)).start(), there)
        got[own_block(n, rows_at(me)), :] = send[own_block(n, me), :]

    def send_bwd(n):
        for mine in (0, 1):

            @pl.when(core == mine)
            def _():
                for there in (0, 1):
                    all_tiles(lambda d: bwd(n, d, rows_of(n, mine)).start(), there)

        got2[own_block(n, me), :] = send2[own_block(n, rows_at(me)), :]

    def by_core(act):
        for mine in (0, 1):
            pl.when(core == mine)(lambda: act(mine))

    def wait_fwd(n):
        by_core(
            lambda mine: total(
                send, got, fwd_s, fwd_r, n, (TILES - 1) * rows_of(n, mine)
            ).wait_recv()
        )

    def wait_bwd(n):
        by_core(
            lambda mine: total(send2, got2, bwd_s, bwd_r, n, rows_mixed(n, mine)).wait_recv()
        )

    arrange(0)
    send_fwd(0)

    spec_across.wait()
    for j in range(1, 8):
        spec_copy(j).start()

    @pl.when(inside)
    def _():
        cells_outer.wait()

    far_r = obs_far[0:1, :]
    far_r = jnp.where(
        far_r >= 5.0 * LEV, far_r + LEV, jnp.where(far_r >= 4.0 * LEV, far_r + 3.0 * LEV, -1.0)
    )
    one, zero = jnp.float32(1.0), jnp.float32(0.0)

    def hot(spots, size):
        spots = spots.astype(jnp.int32)
        numbers = lax.broadcasted_iota(jnp.int32, (size, SLOTS), 0)
        return jnp.where(numbers == spots, one, zero)

    def read(rows, longitudes, lanes):
        hot_x[:, lanes] = hot(longitudes, LON).astype(jnp.bfloat16)
        at = hot(rows, CELL_ROWS)
        hot_r[:, lanes] = at.astype(jnp.bfloat16)
        parts = split(p[...].reshape(CELL_ROWS, LON))
        picked = dot(parts[0], hot_x[:, lanes]) + dot(parts[1], hot_x[:, lanes])
        return jnp.sum(picked * at, axis=0, keepdims=True)

    found[...] = read(far_r, obs_far[1:2, :], slice(SLOTS, 2 * SLOTS))
    found_outer = misc(FOUND, found, found_far, win, outer)
    pl.when(inside)(lambda: found_outer.start())

    for n in (1, 2):
        arrange(n)
        send_fwd(n)

    depart[...] = read(obs[0:1, :], obs[1:2, :], slice(0, SLOTS))
    pl.when(inside)(lambda: found_outer.wait())
    depart[...] = jnp.where(
        obs[0:1, :] >= 0.0,
        precision[...] * (depart[...] + found_far[...] - innovation[...]),
        0.0,
    )
    depart_outer = misc(DEPART, depart, depart_far, win, outer)
    pl.when(inside)(lambda: depart_outer.start())

    def spec_wait(j):
        there_x, there_c = (xx + j // 2) % 4, (core + j % 2) % 2
        return copy(
            spec.at[there_x, :, there_c],
            spec.at[there_x, :, there_c],
            spec_s.at[j],
            spec_r.at[there_x * 2 + there_c],
            win,
            partner,
        )

    for j in range(1, 8):
        spec_wait(j).wait_recv()
    scale = spec[...].reshape(128, NLAT).T
    for n in range(CHUNKS):
        wait_fwd(n)
        units = range(WIDE[n])
        data = got[PART0[n] : PART0[n] + TILES * SPAN[n], :]
        data = data.reshape(TILES, WIDE[n], EXT, 128)
        x = jnp.concatenate([data[:, u].reshape(TILES * EXT, 128) for u in units], axis=1)
        modal = dot3((ph[...], plo[...]), split(x))
        modal = modal * jnp.concatenate([scale] * WIDE[n], axis=1)
        back = dot3((qh[...], ql[...]), split(modal))
        for u in units:
            unit = back[:, u * 128 : u * 128 + 128].reshape(TILES, EXT, 128)
            for t in range(TILES):
                at = PART0[n] + t * SPAN[n] + u * 8
                send2[at : at + 8, :] = unit[t]
        send_bwd(n)
        if n == 1:
            pl.when(inside)(lambda: depart_outer.wait())
            pushed = jnp.concatenate([depart[...], depart_far[...]], axis=1)
            high, low = split(hot_r[...].astype(jnp.float32) * pushed)
            placed = dot_nt(high, hot_x[...]) + dot_nt(low, hot_x[...])
            force[...] = placed.reshape(EXT, LEV, LON)

    def back_step(get, r):
        cen, east, west = weights(la(r), lo(r), dr(r))
        mine = get(r)
        return (
            cen * mine
            + la(r + 1) * get(r + 1)
            + la(r - 1) * get(r - 1)
            + pltpu.roll(east * mine, 1, 1)
            + pltpu.roll(west * mine, LON - 1, 1)
        )

    passed = [
        misc(
            LAMBDA + n,
            lam.at[pl.ds(EXT * LEVEL0[n], ROWS * DEEP[n]), :],
            six(lam_near, n),
            after,
            after_tile,
        )
        for n in range(CHUNKS)
    ]
    edge = [
        misc(
            FORCE + n,
            force.at[pl.ds(0, 2), pl.ds(LEVEL0[n], DEEP[n]), :],
            force_near.at[:, pl.ds(LEVEL0[n], DEEP[n]), :],
            win,
            partner,
        )
        for n in range(CHUNKS)
    ]

    def receive(n):
        wait_bwd(n)
        for i in range(EXT):
            for quarter in range(4):
                for j in range(len(OWNER[n])):
                    at = EXT * LEVEL0[n] + i * DEEP[n] + j * 8
                    lam[at : at + 8, quarter * 128 : quarter * 128 + 128] = got2[
                        pl.ds(unit_base(i, quarter, n, j), 8, stride=2 * SPAN[n]), :
                    ]
        passed[n].start()
        rows = lam[EXT * LEVEL0[n] : EXT * (LEVEL0[n] + DEEP[n]), :]
        fields = dot3_nt(split(rows), (zh[...], zl[...]))
        fields = keep * fields.reshape(EXT, DEEP[n], LON)
        deep = pl.ds(LEVEL0[n], DEEP[n])
        force[:, deep, :] = fields - force[:, deep, :]
        edge[n].start()

    def adjoint(n):
        edge[n].wait()
        deep = pl.ds(LEVEL0[n], DEEP[n])

        def start(r):
            return force_near[-1 - r, deep, :] if r < 0 else force[r, deep, :]

        for r in range(-1, ROWS + 1):
            mid[r + 1, deep, :] = back_step(start, r)
        for r in range(ROWS):
            p[r, deep, :] = back_step(lambda q: mid[q + 1, deep, :], r)

    def finish(n):
        passed[n].wait()
        deep = pl.ds(LEVEL0[n], DEEP[n])
        rows = lam_near[ROWS * LEVEL0[n] : ROWS * (LEVEL0[n] + DEEP[n]), :]
        fields = dot3_nt(split(rows), (zh[...], zl[...])).reshape(ROWS, DEEP[n], LON)
        for i in range(ROWS):
            out[src(i), deep, :] = fields[i] - p[i, deep, :]

    receive(0)
    adjoint(0)
    receive(1)
    adjoint(1)
    finish(0)
    receive(2)
    finish(1)
    adjoint(2)
    finish(2)

    for n in range(CHUNKS):
        by_core(
            lambda mine: total(send, got, fwd_s, fwd_r, n, rows_mixed(n, mine)).wait_send()
        )
        by_core(
            lambda mine: total(
                send2, got2, bwd_s, bwd_r, n, (TILES - 1) * rows_of(n, mine)
            ).wait_send()
        )
    for j in range(1, 8):
        spec_copy(j).wait_send()


def body(
    increment,
    background,
    lat_diffusion,
    lon_diffusion,
    advection,
    spectrum,
    obs_index,
    obs_count,
    innovation,
    obs_precision,
):
    zonal = two_parts(np.ascontiguousarray(zonal_table().T))
    merid = extended_meridional()
    merid_fwd = two_parts(merid)
    merid_back = two_parts(np.ascontiguousarray(merid.T))
    f32 = jnp.float32
    sems = pltpu.SemaphoreType.DMA
    scratch = [
        ((ROWS * LEV, KEEP), f32),
        ((ROWS * LEV, KEEP), f32),
        ((2, LEV, LON), f32),
        ((8, LON), f32),
        ((8, LON), f32),
        ((8, LON), f32),
        ((2, SLOTS), f32),
        ((2, SLOTS), f32),
        ((1, SLOTS), f32),
        ((1, SLOTS), f32),
        ((1, SLOTS), f32),
        ((1, SLOTS), f32),
        ((4, 2, 2, 8, NLAT), f32),
        ((EXT, LEV, LON), f32),
        ((EXT, LEV, LON), f32),
        ((BLOCKS, 128), f32),
        ((BLOCKS, 128), f32),
        ((LON, 2 * SLOTS), jnp.bfloat16),
        ((CELL_ROWS, 2 * SLOTS), jnp.bfloat16),
        ((EXT * LEV, KEEP), f32),
        ((ROWS * LEV, KEEP), f32),
        ((EXT, LEV, LON), f32),
        ((2, LEV, LON), f32),
    ]
    args = (
        increment[0].transpose(1, 0, 2),
        background.transpose(1, 0, 2),
        lat_diffusion.transpose(1, 0, 2),
        lon_diffusion.transpose(1, 0, 2),
        advection.transpose(1, 0, 2),
        spectrum,
        obs_index,
        obs_count,
        innovation,
        obs_precision,
        *zonal,
        *merid_fwd,
        *merid_back,
    )
    vmem = pl.BlockSpec(memory_space=pltpu.VMEM)
    gradient = pl.pallas_call(
        kernel,
        out_shape=jax.ShapeDtypeStruct((ROWS, LEV, LON), f32),
        in_specs=[vmem] * len(args),
        out_specs=vmem,
        scratch_shapes=[pltpu.VMEM(shape, kind) for shape, kind in scratch]
        + [sems((MISC,)), sems((MISC,)), sems((8,)), sems((8,))]
        + [sems((CHUNKS,))] * 4
        + [pltpu.VMEM((BLOCKS, 128), f32)] * 2,
        compiler_params=pltpu.CompilerParams(
            vmem_limit_bytes=VMEM_LIMIT, collective_id=0, has_side_effects=True
        ),
    )(*args)
    return gradient.transpose(1, 0, 2)[None]


def solution(mesh):
    in_specs = (
        P("win", None, "tile", None),
        P(None, "tile", None),
        P("win", "tile", None),
        P("win", "tile", None),
        P("win", "tile", None),
        P("tile", None),
        P("win", "tile"),
        P("win", "tile"),
        P("win", "tile"),
        P("win", "tile"),
    )
    out_specs = P("win", None, "tile", None)
    return jax.shard_map(body, mesh=mesh, in_specs=in_specs, out_specs=out_specs, check_vma=False)
```
